32 devices in a mesh: ctx: 8 (over z, x), head: 4 (over y, core).
Axes of the slice: x: 2, y: 2, z: 4, core: 2. Of those that a mesh axis runs over, the one named last changes fastest.
Arguments:
- queries: bfloat16 [4096, 64, 128], P(('ctx', 'head')), may hold values from -100 to 100
- keys: bfloat16 [4096, 8, 128], P(('ctx', 'head')), may hold values from -6 to 6
- values: bfloat16 [4096, 8, 128], P(('ctx', 'head')), may hold values from -6 to 6
- outputs: bfloat16 [4096, 64, 128], P(('ctx', 'head')), may hold values from -6 to 6
- out_grad: bfloat16 [4096, 64, 128], P(('ctx', 'head')), may hold values from -6 to 6
- segments: int32 [4096], replicated, may hold values from 0 to 127, never falling along the last dimension, each value on 1 to 128 neighbouring positions
Outputs:
- query_grad: bfloat16 [4096, 64, 128], P(('ctx', 'head'))
- key_grad: bfloat16 [4096, 8, 128], P(('ctx', 'head'))
- value_grad: bfloat16 [4096, 8, 128], P(('ctx', 'head'))
The draws below stay inside these ranges and needn't reach their ends.
Inputs may be any that keep to these rules, and one draw needn't show every extreme that they name: `segments`: the document number never falls along the pack; every document has 1 to 128 tokens and one has exactly 128.
All inputs are finite; a program needn't handle non-finite values.
Results may differ from the reference program's by a relative error of at most 0.007.
Values may be sent and summed in bfloat16 or wider, within the bound.
A program may use at most 128 MiB of HBM per device.

```python
import math
import jax
import jax.numpy as jnp
import numpy as np
from jax import lax

QH = 64
KVH = 8
HD = 128
TOKENS = 4096
DOC_MOST = 128
NDOCS = 128
BLOCK = 512


def draw_pair(key):
    base_key = jax.random.fold_in(key, 7001)
    first, second = jax.random.split(base_key, 2)
    key_rows = jax.random.truncated_normal(first, -4.5, 4.5, (TOKENS, KVH, HD), jnp.float32)
    query_rows = jax.random.truncated_normal(second, -4.5, 4.5, (TOKENS, QH, HD), jnp.float32)
    return (query_rows, key_rows)


def draw_queries(key, part):
    return draw_pair(key)[0].astype(jnp.bfloat16)


def draw_keys(key, part):
    return draw_pair(key)[1].astype(jnp.bfloat16)


def block_levels(stream_key, shape, cuts, low, high):
    def one(position, blocks):
        draws = jax.random.uniform(jax.random.fold_in(jax.random.fold_in(stream_key, 6), position), (blocks,), jnp.float32, low / len(cuts), high / len(cuts))
        return jnp.repeat(jnp.exp(draws), shape[position] // blocks).reshape((-1,) + (1,) * (len(shape) - position - 1))

    level = one(*cuts[0])
    for cut in cuts[1:]:
        level = level * one(*cut)
    return level


def length_profile(number_of, total, bound, slope):
    weights = [(1 << 20) // math.isqrt(rank ** slope) + 1 for rank in range(2, number_of + 1)]
    spare, counts = total - bound - (number_of - 1), [1] * (number_of - 1)
    while spare > 0:
        free = [i for i in range(number_of - 1) if counts[i] < bound]
        mass, budget = sum([weights[i] for i in free]), spare
        for i in free:
            more = min(bound - counts[i], max(1, budget * weights[i] // mass), spare)
            counts[i] = counts[i] + more
            spare = spare - more
    return np.array([bound] + counts)


def uneven_parts(own_key, amount, total, reach, skew):
    if amount == 2:
        one = jax.random.randint(own_key, (), max(1, total - reach), min(reach, total - 1) + 1)
        return jnp.stack([one, total - one])
    tallies = jnp.asarray(length_profile(amount, total, reach, skew), jnp.int32)
    twos = (amount - 1) // 2
    donor, taker = tallies[1:1 + 2 * twos:2], tallies[2:2 + 2 * twos:2]
    margin = jnp.minimum(donor - 1, reach - taker)
    passed = jax.random.randint(jax.random.fold_in(own_key, 1), (twos,), 0, 1 << 20) % (margin + 1)
    tallies = tallies.at[1:1 + 2 * twos:2].set(donor - passed).at[2:2 + 2 * twos:2].set(taker + passed)
    return tallies[jax.random.permutation(jax.random.fold_in(own_key, 2), amount)]


def normal_values(own_key, extent, scale, limit, shards=(), held_as=jnp.bfloat16):
    gain = block_levels(own_key, extent, shards, -0.22, 0.18) if shards else 1.0
    values = jax.random.normal(own_key, extent, jnp.float32) * scale * gain
    return jnp.minimum(jnp.maximum(values, -limit), limit).astype(held_as)


def setup_inputs(seed: int = 0) -> dict:
    streams_of = jax.random.split(jax.random.key(seed), 7)
    queries = draw_queries(jax.random.fold_in(streams_of[6], 71), 0)
    keys = draw_keys(jax.random.fold_in(streams_of[6], 71), 0)
    values = normal_values(streams_of[2], (TOKENS, KVH, HD), 1.0, 6.0, ((0, 32),))
    outputs = normal_values(streams_of[3], (TOKENS, QH, HD), 1.0, 6.0, ((0, 32),))
    out_grad = normal_values(streams_of[4], (TOKENS, QH, HD), 1.0, 6.0, ((0, 32),))
    segments = jnp.searchsorted(jnp.cumsum(uneven_parts(streams_of[5], NDOCS, TOKENS, DOC_MOST, 2)), jnp.arange(TOKENS), side="right").astype(jnp.int32)
    return dict(queries=queries, keys=keys, values=values, outputs=outputs, out_grad=out_grad, segments=segments)


def reference(queries, keys, values, outputs, out_grad, segments):
    group = QH // KVH
    scale = HD ** -0.5
    window = DOC_MOST + BLOCK
    delta_all = jnp.sum(out_grad.astype(jnp.float32) * outputs.astype(jnp.float32), axis=2)
    keys_pad = jnp.concatenate([jnp.zeros((DOC_MOST, KVH, HD), keys.dtype), keys], axis=0)
    values_pad = jnp.concatenate([jnp.zeros((DOC_MOST, KVH, HD), values.dtype), values], axis=0)
    seg_pad = jnp.concatenate([jnp.full((DOC_MOST,), -1, jnp.int32), segments.astype(jnp.int32)], axis=0)
    row_index = jnp.arange(BLOCK, dtype=jnp.int32)
    col_index = jnp.arange(window, dtype=jnp.int32)
    causal = col_index[None, :] <= row_index[:, None] + DOC_MOST

    def one_block(carry, block_index):
        grad_keys, grad_values = carry
        start_row = (block_index * BLOCK).astype(jnp.int32)
        q_block = lax.dynamic_slice_in_dim(queries, start_row, BLOCK, 0).reshape(BLOCK, KVH, group, HD)
        g_block = lax.dynamic_slice_in_dim(out_grad, start_row, BLOCK, 0).reshape(BLOCK, KVH, group, HD)
        d_block = lax.dynamic_slice_in_dim(delta_all, start_row, BLOCK, 0).reshape(BLOCK, KVH, group)
        d_block = jnp.transpose(d_block, (1, 2, 0))
        k_window = lax.dynamic_slice_in_dim(keys_pad, start_row, window, 0)
        v_window = lax.dynamic_slice_in_dim(values_pad, start_row, window, 0)
        seg_query = lax.dynamic_slice_in_dim(segments.astype(jnp.int32), start_row, BLOCK, 0)
        seg_keys = lax.dynamic_slice_in_dim(seg_pad, start_row, window, 0)
        allowed = (seg_query[:, None] == seg_keys[None, :]) & causal
        raw = scale * jnp.einsum("bkgd,wkd->kgbw", q_block.astype(jnp.float32), k_window.astype(jnp.float32))
        masked = jnp.where(allowed, raw, -jnp.inf)
        top = jnp.max(masked, axis=-1)
        log_sum = top + jnp.log(jnp.sum(jnp.exp(masked - top[..., None]), axis=-1))
        prob = jnp.exp(masked - log_sum[..., None])
        prob_low = prob.astype(jnp.bfloat16)
        d_prob = jnp.einsum("bkgd,wkd->kgbw", g_block.astype(jnp.float32), v_window.astype(jnp.float32))
        d_score = (prob * (d_prob - d_block[..., None])).astype(jnp.bfloat16)
        query_part = scale * jnp.einsum("kgbw,wkd->bkgd", d_score.astype(jnp.float32), k_window.astype(jnp.float32))
        key_part = scale * jnp.einsum("kgbw,bkgd->wkd", d_score.astype(jnp.float32), q_block.astype(jnp.float32))
        value_part = jnp.einsum("kgbw,bkgd->wkd", prob_low.astype(jnp.float32), g_block.astype(jnp.float32))
        old_keys = lax.dynamic_slice_in_dim(grad_keys, start_row, window, 0)
        old_values = lax.dynamic_slice_in_dim(grad_values, start_row, window, 0)
        grad_keys = lax.dynamic_update_slice_in_dim(grad_keys, old_keys + key_part, start_row, 0)
        grad_values = lax.dynamic_update_slice_in_dim(grad_values, old_values + value_part, start_row, 0)
        return (grad_keys, grad_values), query_part.reshape(BLOCK, QH, HD).astype(jnp.bfloat16)

    start_keys = jnp.zeros((TOKENS + DOC_MOST, KVH, HD), jnp.float32)
    start_values = jnp.zeros((TOKENS + DOC_MOST, KVH, HD), jnp.float32)
    (grad_keys, grad_values), query_blocks = lax.scan(one_block, (start_keys, start_values), jnp.arange(TOKENS // BLOCK, dtype=jnp.int32))
    query_grad = query_blocks.reshape(TOKENS, QH, HD)
    return query_grad, grad_keys[DOC_MOST:].astype(jnp.bfloat16), grad_values[DOC_MOST:].astype(jnp.bfloat16)
```

```python
import functools
import math

import jax
import jax.numpy as jnp
from jax import lax
from jax.experimental import pallas as pl
from jax.experimental.pallas import tpu as pltpu
from jax.sharding import PartitionSpec as P

SUB = 32
MASKED = -1e30
MESH = pl.DeviceIdType.MESH


def nt(a, b):
    return lax.dot_general(a, b, (((1,), (1,)), ((), ())), preferred_element_type=jnp.float32)


def nn(a, b):
    return jnp.dot(a, b, preferred_element_type=jnp.float32)


def tn(a, b):
    return lax.dot_general(a, b, (((0,), (0,)), ((), ())), preferred_element_type=jnp.float32)


def kernel(
    sizes,
    q_hbm, k_ref, v_ref, o_hbm, g_hbm, seg_ref,
    dq_hbm, dk_ref, dv_ref,
    q_buf, g_buf, o_buf, dq_buf, flat, kv_own, kv_prev, back_out, back_in, own_sum, bias,
    in_sem, dq_sem, fwd_send, fwd_recv, bwd_send, bwd_recv,
):
    ctx_count, head_count, halo, rows, kv_heads, group, dim = sizes
    devices = ctx_count * head_count
    span = halo * rows
    pairs = kv_heads // 2
    wide = 2 * group
    lanes = SUB * group
    width = span + SUB
    parts = rows // SUB
    scale = dim ** (-0.5)
    me = lax.axis_index("ctx") * head_count + lax.axis_index("head")

    def device(i):
        return (i // head_count, i % head_count)

    def load(number, hbm, buf, jj):
        return pltpu.make_async_copy(
            hbm.at[:, pl.ds(jj * wide, wide), :], buf.at[jj], in_sem.at[number, jj]
        )

    def store(jj):
        return pltpu.make_async_copy(
            dq_buf.at[jj], dq_hbm.at[:, pl.ds(jj * wide, wide), :], dq_sem.at[jj]
        )

    def forward(h, jj):
        return pltpu.make_async_remote_copy(
            src_ref=kv_own.at[jj], dst_ref=kv_prev.at[h - 1, jj],
            send_sem=fwd_send.at[h - 1, jj], recv_sem=fwd_recv.at[h - 1, jj],
            device_id=device(me + h), device_id_type=MESH,
        )

    def backward(h, jj):
        return pltpu.make_async_remote_copy(
            src_ref=back_out.at[h - 1, jj], dst_ref=back_in.at[h - 1, jj],
            send_sem=bwd_send.at[h - 1, jj], recv_sem=bwd_recv.at[h - 1, jj],
            device_id=device(me - h), device_id_type=MESH,
        )

    barrier = pltpu.get_barrier_semaphore()
    for h in range(1, halo + 1):
        @pl.when(me >= h)
        def _():
            pl.semaphore_signal(barrier, inc=1, device_id=device(me - h), device_id_type=MESH)

        @pl.when(me + h < devices)
        def _():
            pl.semaphore_signal(barrier, inc=1, device_id=device(me + h), device_id_type=MESH)

    for jj in range(pairs):
        load(0, q_hbm, q_buf, jj).start()
        load(1, g_hbm, g_buf, jj).start()
        load(2, o_hbm, o_buf, jj).start()

    flat[0] = k_ref[...].astype(jnp.float32).reshape(rows * kv_heads, dim)
    flat[1] = v_ref[...].astype(jnp.float32).reshape(rows * kv_heads, dim)

    def split(jj):
        for c in range(2):
            for which in range(2):
                kv_own[jj, 2 * c + which] = flat[
                    which, pl.ds(2 * jj + c, rows, stride=kv_heads), :
                ].astype(jnp.bfloat16)

    split(0)
    pl.semaphore_wait(barrier, jnp.minimum(me, halo) + jnp.minimum(devices - 1 - me, halo))

    for jj in range(pairs):
        if jj:
            split(jj)
        for h in range(1, halo + 1):
            @pl.when(me + h < devices)
            def _():
                forward(h, jj).start()

    for h in range(1, halo + 1):
        @pl.when(me < h)
        def _():
            kv_prev[h - 1] = jnp.zeros(kv_prev.shape[1:], kv_prev.dtype)

    token = lax.broadcasted_iota(jnp.int32, (rows, rows * group), 0)
    lane = lax.broadcasted_iota(jnp.int32, (rows, rows * group), 1)
    spread = jnp.where(lane // group == token, 1.0, 0.0).astype(jnp.bfloat16)
    own_seg = seg_ref[pl.ds(me, 1), :].astype(jnp.float32)
    seg_query = nn(jnp.broadcast_to(own_seg, (8, rows)).astype(jnp.bfloat16), spread)[0:1]
    diagonal = lax.broadcasted_iota(jnp.int32, (rows, rows), 0) == lax.broadcasted_iota(
        jnp.int32, (rows, rows), 1
    )
    ones = jnp.ones((rows, lanes), jnp.bfloat16)
    columns = []
    for h in range(halo, -1, -1):
        line = seg_ref[pl.ds(jnp.maximum(me - h, 0), 1), :].astype(jnp.float32)
        line = jnp.where(me >= h, line, -1.0)
        column = jnp.where(diagonal, jnp.broadcast_to(line, (rows, rows)), 0.0)
        columns.append(nn(column.astype(jnp.bfloat16), ones))
    seg_key = jnp.concatenate(columns, axis=0)
    key_row = lax.broadcasted_iota(jnp.int32, (width, lanes), 0)
    query_row = lax.broadcasted_iota(jnp.int32, (width, lanes), 1) // group
    causal = key_row <= query_row + span
    for a in range(parts):
        same = seg_key[a * SUB : a * SUB + width] == seg_query[:, a * lanes : (a + 1) * lanes]
        bias[a] = jnp.where(same & causal, 0.0, MASKED)

    def pair(jj, _):
        load(0, q_hbm, q_buf, jj).wait()
        load(1, g_hbm, g_buf, jj).wait()
        load(2, o_hbm, o_buf, jj).wait()
        for h in range(1, halo + 1):
            @pl.when(me >= h)
            def _():
                forward(h, jj).wait_recv()

        q_pair = q_buf[jj].astype(jnp.float32)
        g_pair = g_buf[jj].astype(jnp.float32)
        o_pair = o_buf[jj].astype(jnp.float32)
        dq_pair = []
        for c in range(2):
            heads = slice(c * group, (c + 1) * group)
            q = q_pair[:, heads, :].reshape(rows * group, dim).astype(jnp.bfloat16)
            g_wide = g_pair[:, heads, :].reshape(rows * group, dim)
            g = g_wide.astype(jnp.bfloat16)
            product = g_wide * o_pair[:, heads, :].reshape(rows * group, dim)
            high = product.astype(jnp.bfloat16)
            low = (product - high.astype(jnp.float32)).astype(jnp.bfloat16)
            one = jnp.ones((8, dim), jnp.bfloat16)
            delta = (nt(one, high) + nt(one, low))[0:1]
            k = jnp.concatenate(
                [kv_prev[h - 1, jj, 2 * c] for h in range(halo, 0, -1)] + [kv_own[jj, 2 * c]], axis=0
            )
            v = jnp.concatenate(
                [kv_prev[h - 1, jj, 2 * c + 1] for h in range(halo, 0, -1)] + [kv_own[jj, 2 * c + 1]],
                axis=0,
            )
            pieces = (span + rows) // SUB
            dk = [None] * pieces
            dv = [None] * pieces
            dq = []
            for a in range(parts):
                q_a = q[a * lanes : (a + 1) * lanes]
                g_a = g[a * lanes : (a + 1) * lanes]
                k_a = k[a * SUB : a * SUB + width]
                v_a = v[a * SUB : a * SUB + width]
                raw = nt(k_a, q_a) + bias[a]
                top = jnp.max(raw, axis=0, keepdims=True)
                e = jnp.exp2((raw - top) * (scale * math.log2(math.e)))
                prob = e * (1.0 / jnp.sum(e, axis=0, keepdims=True))
                d_prob = nt(v_a, g_a)
                d_score = (prob * (d_prob - delta[:, a * lanes : (a + 1) * lanes])).astype(jnp.bfloat16)
                dv_a = nn(prob.astype(jnp.bfloat16), g_a)
                dk_a = nn(d_score, q_a)
                dq.append(tn(d_score, k_a) * scale)
                for b in range(width // SUB):
                    at = slice(b * SUB, (b + 1) * SUB)
                    dk[a + b] = dk_a[at] if dk[a + b] is None else dk[a + b] + dk_a[at]
                    dv[a + b] = dv_a[at] if dv[a + b] is None else dv[a + b] + dv_a[at]
            dq_pair.append(jnp.concatenate(dq, axis=0).reshape(rows, group, dim))
            for h in range(halo, -1, -1):
                at = slice((halo - h) * parts, (halo - h + 1) * parts)
                dk_h = jnp.concatenate(dk[at], axis=0) * scale
                dv_h = jnp.concatenate(dv[at], axis=0)
                if h:
                    back_out[h - 1, jj, 2 * c] = dk_h.astype(jnp.bfloat16)
                    back_out[h - 1, jj, 2 * c + 1] = dv_h.astype(jnp.bfloat16)
                else:
                    own_sum[jj, 2 * c] = dk_h
                    own_sum[jj, 2 * c + 1] = dv_h
        dq_buf[jj] = jnp.concatenate(dq_pair, axis=1).astype(jnp.bfloat16)
        store(jj).start()
        for h in range(1, halo + 1):
            @pl.when(me >= h)
            def _():
                backward(h, jj).start()
        return 0

    lax.fori_loop(0, pairs, pair, 0)

    for jj in range(pairs):
        for h in range(1, halo + 1):
            @pl.when(me + h < devices)
            def _():
                backward(h, jj).wait_recv()
                own_sum[jj] = own_sum[jj] + back_in[h - 1, jj].astype(jnp.float32)
        for c in range(2):
            for which in range(2):
                flat[which, pl.ds(2 * jj + c, rows, stride=kv_heads), :] = own_sum[jj, 2 * c + which]
    dk_ref[...] = flat[0].reshape(rows, kv_heads, dim).astype(jnp.bfloat16)
    dv_ref[...] = flat[1].reshape(rows, kv_heads, dim).astype(jnp.bfloat16)

    for jj in range(pairs):
        store(jj).wait()
        for h in range(1, halo + 1):
            @pl.when(me + h < devices)
            def _():
                forward(h, jj).wait_send()

            @pl.when(me >= h)
            def _():
                backward(h, jj).wait_send()


def shards(queries, keys, values, outputs, out_grad, segments):
    ctx_count, head_count = lax.axis_size("ctx"), lax.axis_size("head")
    rows, q_heads, dim = queries.shape
    kv_heads = keys.shape[1]
    group = q_heads // kv_heads
    halo = max(1, head_count // 4)
    pairs = kv_heads // 2
    width = halo * rows + SUB
    sizes = (ctx_count, head_count, halo, rows, kv_heads, group, dim)
    lines = segments.reshape(ctx_count * head_count, rows)
    bf16, f32 = jnp.bfloat16, jnp.float32
    big = pltpu.VMEM((pairs, rows, 2 * group, dim), bf16)
    vmem = pl.BlockSpec(memory_space=pltpu.VMEM)
    hbm = pl.BlockSpec(memory_space=pl.ANY)
    work = rows * q_heads * (halo + 1) * rows
    return pl.pallas_call(
        functools.partial(kernel, sizes),
        out_shape=(
            jax.ShapeDtypeStruct(queries.shape, bf16),
            jax.ShapeDtypeStruct(keys.shape, bf16),
            jax.ShapeDtypeStruct(values.shape, bf16),
        ),
        in_specs=[hbm, vmem, vmem, hbm, hbm, vmem],
        out_specs=(hbm, vmem, vmem),
        scratch_shapes=[
            big, big, big, big,
            pltpu.VMEM((2, rows * kv_heads, dim), f32),
            pltpu.VMEM((pairs, 4, rows, dim), bf16),
            pltpu.VMEM((halo, pairs, 4, rows, dim), bf16),
            pltpu.VMEM((halo, pairs, 4, rows, dim), bf16),
            pltpu.VMEM((halo, pairs, 4, rows, dim), bf16),
            pltpu.VMEM((pairs, 4, rows, dim), f32),
            pltpu.VMEM((rows // SUB, width, SUB * group), f32),
            pltpu.SemaphoreType.DMA((3, pairs)),
            pltpu.SemaphoreType.DMA((pairs,)),
            pltpu.SemaphoreType.DMA((halo, pairs)),
            pltpu.SemaphoreType.DMA((halo, pairs)),
            pltpu.SemaphoreType.DMA((halo, pairs)),
            pltpu.SemaphoreType.DMA((halo, pairs)),
        ],
        compiler_params=pltpu.CompilerParams(
            collective_id=0, has_side_effects=True, vmem_limit_bytes=48 * 1024 * 1024
        ),
        cost_estimate=pl.CostEstimate(
            flops=10 * work * dim, bytes_accessed=8 * rows * q_heads * dim, transcendentals=work
        ),
    )(queries, keys, values, outputs, out_grad, lines)


def solution(mesh):
    tokens = P(("ctx", "head"), None, None)
    return jax.shard_map(
        shards,
        mesh=mesh,
        in_specs=(tokens, tokens, tokens, tokens, tokens, P()),
        out_specs=(tokens, tokens, tokens),
        check_vma=False,
    )
```

```python
import functools
import math

import jax
import jax.numpy as jnp
from jax import lax
from jax.experimental import pallas as pl
from jax.experimental.pallas import tpu as pltpu
from jax.sharding import PartitionSpec as P

SUB = 32
MASKED = -1e30
MESH = pl.DeviceIdType.MESH


def nt(a, b):
    return lax.dot_general(a, b, (((1,), (1,)), ((), ())), preferred_element_type=jnp.float32)


def nn(a, b):
    return jnp.dot(a, b, preferred_element_type=jnp.float32)


def tn(a, b):
    return lax.dot_general(a, b, (((0,), (0,)), ((), ())), preferred_element_type=jnp.float32)


def kernel(
    sizes,
    q_hbm, k_hbm, v_hbm, o_hbm, g_hbm, seg_hbm,
    dq_hbm, dk_hbm, dv_hbm,
    q_buf, g_buf, o_buf, dq_buf, kv_raw, seg_ref, flat, kv_own, kv_prev, back_out, back_in, own_sum, bias,
    in_sem, dq_sem, kv_sem, fwd_send, fwd_recv, bwd_send, bwd_recv,
):
    ctx_count, head_count, halo, rows, kv_heads, group, dim = sizes
    devices = ctx_count * head_count
    span = halo * rows
    pairs = kv_heads // 2
    wide = 2 * group
    lanes = SUB * group
    width = span + SUB
    parts = rows // SUB
    scale = dim ** (-0.5)
    me = lax.axis_index("ctx") * head_count + lax.axis_index("head")

    def device(i):
        return (i // head_count, i % head_count)

    def load(number, hbm, buf, jj):
        return pltpu.make_async_copy(
            hbm.at[:, pl.ds(jj * wide, wide), :], buf.at[jj], in_sem.at[number, jj]
        )

    def store(jj):
        return pltpu.make_async_copy(dq_buf.at[jj], dq_hbm.at[jj], dq_sem.at[jj])

    def forward(h, jj):
        return pltpu.make_async_remote_copy(
            src_ref=kv_own.at[jj], dst_ref=kv_prev.at[h - 1, jj],
            send_sem=fwd_send.at[h - 1, jj], recv_sem=fwd_recv.at[h - 1, jj],
            device_id=device(me + h), device_id_type=MESH,
        )

    def backward(h, jj):
        return pltpu.make_async_remote_copy(
            src_ref=back_out.at[h - 1, jj], dst_ref=back_in.at[h - 1, jj],
            send_sem=bwd_send.at[h - 1, jj], recv_sem=bwd_recv.at[h - 1, jj],
            device_id=device(me - h), device_id_type=MESH,
        )

    first = [
        pltpu.make_async_copy(k_hbm, kv_raw.at[0], kv_sem.at[0]),
        pltpu.make_async_copy(v_hbm, kv_raw.at[1], kv_sem.at[1]),
        pltpu.make_async_copy(seg_hbm, seg_ref, kv_sem.at[2]),
    ]
    for copy in first:
        copy.start()
    barrier = pltpu.get_barrier_semaphore()
    for h in range(1, halo + 1):
        @pl.when(me >= h)
        def _():
            pl.semaphore_signal(barrier, inc=1, device_id=device(me - h), device_id_type=MESH)

        @pl.when(me + h < devices)
        def _():
            pl.semaphore_signal(barrier, inc=1, device_id=device(me + h), device_id_type=MESH)

    for jj in range(pairs):
        load(0, q_hbm, q_buf, jj).start()
        load(1, g_hbm, g_buf, jj).start()
        load(2, o_hbm, o_buf, jj).start()

    for which in range(2):
        first[which].wait()
        flat[which] = kv_raw[which].astype(jnp.float32).reshape(rows * kv_heads, dim)

    def split(jj):
        for c in range(2):
            for which in range(2):
                kv_own[jj, 2 * c + which] = flat[
                    which, pl.ds(2 * jj + c, rows, stride=kv_heads), :
                ].astype(jnp.bfloat16)

    split(0)
    pl.semaphore_wait(barrier, jnp.minimum(me, halo) + jnp.minimum(devices - 1 - me, halo))

    for jj in range(pairs):
        if jj:
            split(jj)
        for h in range(1, halo + 1):
            @pl.when(me + h < devices)
            def _():
                forward(h, jj).start()

    for h in range(1, halo + 1):
        @pl.when(me < h)
        def _():
            kv_prev[h - 1] = jnp.zeros(kv_prev.shape[1:], kv_prev.dtype)

    first[2].wait()
    token = lax.broadcasted_iota(jnp.int32, (rows, rows * group), 0)
    lane = lax.broadcasted_iota(jnp.int32, (rows, rows * group), 1)
    spread = jnp.where(lane // group == token, 1.0, 0.0).astype(jnp.bfloat16)
    own_seg = seg_ref[pl.ds(me, 1), :].astype(jnp.float32)
    seg_query = nn(jnp.broadcast_to(own_seg, (8, rows)).astype(jnp.bfloat16), spread)[0:1]
    diagonal = lax.broadcasted_iota(jnp.int32, (rows, rows), 0) == lax.broadcasted_iota(
        jnp.int32, (rows, rows), 1
    )
    ones = jnp.ones((rows, lanes), jnp.bfloat16)
    columns = []
    for h in range(halo, -1, -1):
        line = seg_ref[pl.ds(jnp.maximum(me - h, 0), 1), :].astype(jnp.float32)
        line = jnp.where(me >= h, line, -1.0)
        column = jnp.where(diagonal, jnp.broadcast_to(line, (rows, rows)), 0.0)
        columns.append(nn(column.astype(jnp.bfloat16), ones))
    seg_key = jnp.concatenate(columns, axis=0)
    key_row = lax.broadcasted_iota(jnp.int32, (width, lanes), 0)
    query_row = lax.broadcasted_iota(jnp.int32, (width, lanes), 1) // group
    causal = key_row <= query_row + span
    for a in range(parts):
        same = seg_key[a * SUB : a * SUB + width] == seg_query[:, a * lanes : (a + 1) * lanes]
        bias[a] = jnp.where(same & causal, 0.0, MASKED)

    low_half = lax.broadcasted_iota(jnp.int32, (rows * group, dim), 1) < dim // 2

    def pair(jj, _):
        load(0, q_hbm, q_buf, jj).wait()
        load(1, g_hbm, g_buf, jj).wait()
        load(2, o_hbm, o_buf, jj).wait()
        for h in range(1, halo + 1):
            @pl.when(me >= h)
            def _():
                forward(h, jj).wait_recv()

        q_pair = q_buf[jj].astype(jnp.float32)
        g_pair = g_buf[jj].astype(jnp.float32)
        o_pair = o_buf[jj].astype(jnp.float32)
        dq_pair = []
        for c in range(2):
            heads = slice(c * group, (c + 1) * group)
            q = q_pair[:, heads, :].reshape(rows * group, dim).astype(jnp.bfloat16)
            g_wide = g_pair[:, heads, :].reshape(rows * group, dim)
            g = g_wide.astype(jnp.bfloat16)
            product = g_wide * o_pair[:, heads, :].reshape(rows * group, dim)
            product = product + pltpu.roll(product, dim // 2, 1)
            high = product.astype(jnp.bfloat16).astype(jnp.float32)
            terms = jnp.where(low_half, high, product - high).astype(jnp.bfloat16)
            g_terms = jnp.concatenate([g, terms], axis=1)
            k = jnp.concatenate(
                [kv_prev[h - 1, jj, 2 * c] for h in range(halo, 0, -1)] + [kv_own[jj, 2 * c]], axis=0
            )
            v = jnp.concatenate(
                [kv_prev[h - 1, jj, 2 * c + 1] for h in range(halo, 0, -1)] + [kv_own[jj, 2 * c + 1]],
                axis=0,
            )
            v = jnp.concatenate([v, jnp.full(v.shape, -1.0, v.dtype)], axis=1)
            pieces = (span + rows) // SUB
            dk = [None] * pieces
            dv = [None] * pieces
            dq = []
            for a in range(parts):
                q_a = q[a * lanes : (a + 1) * lanes]
                g_a = g[a * lanes : (a + 1) * lanes]
                k_a = k[a * SUB : a * SUB + width]
                v_a = v[a * SUB : a * SUB + width]
                raw = nt(k_a, q_a) + bias[a]
                top = jnp.max(raw, axis=0, keepdims=True)
                e = jnp.exp2((raw - top) * (scale * math.log2(math.e)))
                prob = e * (1.0 / jnp.sum(e, axis=0, keepdims=True))
                d_prob = nt(v_a, g_terms[a * lanes : (a + 1) * lanes])
                d_score = (prob * d_prob).astype(jnp.bfloat16)
                dv_a = nn(prob.astype(jnp.bfloat16), g_a)
                dk_a = nn(d_score, q_a)
                dq.append(tn(d_score, k_a) * scale)
                for b in range(width // SUB):
                    at = slice(b * SUB, (b + 1) * SUB)
                    dk[a + b] = dk_a[at] if dk[a + b] is None else dk[a + b] + dk_a[at]
                    dv[a + b] = dv_a[at] if dv[a + b] is None else dv[a + b] + dv_a[at]
            dq_pair.append(jnp.concatenate(dq, axis=0).reshape(rows, group, dim))
            for h in range(halo, -1, -1):
                at = slice((halo - h) * parts, (halo - h + 1) * parts)
                dk_h = jnp.concatenate(dk[at], axis=0) * scale
                dv_h = jnp.concatenate(dv[at], axis=0)
                if h:
                    back_out[h - 1, jj, 2 * c] = dk_h.astype(jnp.bfloat16)
                    back_out[h - 1, jj, 2 * c + 1] = dv_h.astype(jnp.bfloat16)
                else:
                    own_sum[jj, 2 * c] = dk_h
                    own_sum[jj, 2 * c + 1] = dv_h
        dq_buf[jj] = jnp.concatenate(dq_pair, axis=1).astype(jnp.bfloat16)
        store(jj).start()
        for h in range(1, halo + 1):
            @pl.when(me >= h)
            def _():
                backward(h, jj).start()
        return 0

    lax.fori_loop(0, pairs, pair, 0)

    for jj in range(pairs):
        for h in range(1, halo + 1):
            @pl.when(me + h < devices)
            def _():
                backward(h, jj).wait_recv()
                own_sum[jj] = own_sum[jj] + back_in[h - 1, jj].astype(jnp.float32)
        for c in range(2):
            for which in range(2):
                flat[which, pl.ds(2 * jj + c, rows, stride=kv_heads), :] = own_sum[jj, 2 * c + which]
    last = [
        pltpu.make_async_copy(kv_raw.at[0], dk_hbm, kv_sem.at[0]),
        pltpu.make_async_copy(kv_raw.at[1], dv_hbm, kv_sem.at[1]),
    ]
    for which in range(2):
        kv_raw[which] = flat[which].reshape(rows, kv_heads, dim).astype(jnp.bfloat16)
        last[which].start()

    for jj in range(pairs):
        store(jj).wait()
        for h in range(1, halo + 1):
            @pl.when(me + h < devices)
            def _():
                forward(h, jj).wait_send()

            @pl.when(me >= h)
            def _():
                backward(h, jj).wait_send()
    for copy in last:
        copy.wait()


def write(dq_ref, dk_ref, dv_ref, dq_hbm, dk_hbm, dv_hbm, sem):
    pairs, _, wide, _ = dq_ref.shape
    copies = [
        pltpu.make_async_copy(dq_ref.at[jj], dq_hbm.at[:, pl.ds(jj * wide, wide), :], sem.at[jj])
        for jj in range(pairs)
    ]
    copies.append(pltpu.make_async_copy(dk_ref, dk_hbm, sem.at[pairs]))
    copies.append(pltpu.make_async_copy(dv_ref, dv_hbm, sem.at[pairs + 1]))
    for copy in copies:
        copy.start()
    for copy in copies:
        copy.wait()


def shards(queries, keys, values, outputs, out_grad, segments):
    ctx_count, head_count = lax.axis_size("ctx"), lax.axis_size("head")
    rows, q_heads, dim = queries.shape
    kv_heads = keys.shape[1]
    group = q_heads // kv_heads
    halo = max(1, head_count // 4)
    pairs = kv_heads // 2
    width = halo * rows + SUB
    sizes = (ctx_count, head_count, halo, rows, kv_heads, group, dim)
    lines = segments.reshape(ctx_count * head_count, rows)
    bf16, f32 = jnp.bfloat16, jnp.float32
    big = pltpu.VMEM((pairs, rows, 2 * group, dim), bf16)
    hbm = pl.BlockSpec(memory_space=pl.ANY)
    limit = 56 * 1024 * 1024
    work = rows * q_heads * (halo + 1) * rows
    shapes = (
        jax.ShapeDtypeStruct(queries.shape, bf16),
        jax.ShapeDtypeStruct(keys.shape, bf16),
        jax.ShapeDtypeStruct(values.shape, bf16),
    )
    grads = pl.pallas_call(
        functools.partial(kernel, sizes),
        out_shape=(
            jax.ShapeDtypeStruct((pairs, rows, 2 * group, dim), bf16),
            jax.ShapeDtypeStruct(keys.shape, bf16),
            jax.ShapeDtypeStruct(values.shape, bf16),
        ),
        in_specs=[hbm] * 6,
        out_specs=(hbm,) * 3,
        scratch_shapes=[
            big, big, big, big,
            pltpu.VMEM((2, rows, kv_heads, dim), bf16),
            pltpu.VMEM(lines.shape, jnp.int32),
            pltpu.VMEM((2, rows * kv_heads, dim), f32),
            pltpu.VMEM((pairs, 4, rows, dim), bf16),
            pltpu.VMEM((halo, pairs, 4, rows, dim), bf16),
            pltpu.VMEM((halo, pairs, 4, rows, dim), bf16),
            pltpu.VMEM((halo, pairs, 4, rows, dim), bf16),
            pltpu.VMEM((pairs, 4, rows, dim), f32),
            pltpu.VMEM((rows // SUB, width, SUB * group), f32),
            pltpu.SemaphoreType.DMA((3, pairs)),
            pltpu.SemaphoreType.DMA((pairs,)),
            pltpu.SemaphoreType.DMA((3,)),
            pltpu.SemaphoreType.DMA((halo, pairs)),
            pltpu.SemaphoreType.DMA((halo, pairs)),
            pltpu.SemaphoreType.DMA((halo, pairs)),
            pltpu.SemaphoreType.DMA((halo, pairs)),
        ],
        compiler_params=pltpu.CompilerParams(
            collective_id=0, has_side_effects=True, vmem_limit_bytes=limit
        ),
        cost_estimate=pl.CostEstimate(
            flops=10 * work * dim, bytes_accessed=8 * rows * q_heads * dim, transcendentals=work
        ),
    )(queries, keys, values, outputs, out_grad, lines)
    return pl.pallas_call(
        write,
        out_shape=shapes,
        in_specs=[hbm] * 3,
        out_specs=(hbm,) * 3,
        scratch_shapes=[pltpu.SemaphoreType.DMA((pairs + 2,))],
        compiler_params=pltpu.CompilerParams(vmem_limit_bytes=limit),
    )(*grads)


def solution(mesh):
    tokens = P(("ctx", "head"), None, None)
    return jax.shard_map(
        shards,
        mesh=mesh,
        in_specs=(tokens, tokens, tokens, tokens, tokens, P()),
        out_specs=(tokens, tokens, tokens),
        check_vma=False,
    )
```

```python
import functools
import math

import jax
import jax.numpy as jnp
from jax import lax
from jax.experimental import pallas as pl
from jax.experimental.pallas import tpu as pltpu
from jax.sharding import PartitionSpec as P

SUB = 32
PARTS = 8
MASKED = -1e30
MESH = pl.DeviceIdType.MESH


def nt(a, b):
    return lax.dot_general(a, b, (((1,), (1,)), ((), ())), preferred_element_type=jnp.float32)


def nn(a, b):
    return jnp.dot(a, b, preferred_element_type=jnp.float32)


def tn(a, b):
    return lax.dot_general(a, b, (((0,), (0,)), ((), ())), preferred_element_type=jnp.float32)


def kernel(
    sizes,
    q_hbm, k_hbm, v_hbm, o_hbm, g_hbm, seg_hbm,
    dq_hbm, dk_hbm, dv_hbm,
    q_buf, g_buf, o_buf, dq_buf, kv_raw, seg_ref, flat, kv_own, kv_prev, back_out, back_in, own_sum, bias,
    in_sem, dq_sem, kv_sem, fwd_send, fwd_recv, bwd_send, bwd_recv,
):
    ctx_count, head_count, halo, rows, kv_heads, group, dim = sizes
    devices = ctx_count * head_count
    span = halo * rows
    pairs = kv_heads // 2
    wide = 2 * group
    lanes = SUB * group
    width = span + SUB
    parts = rows // SUB
    scale = dim ** (-0.5)
    me = lax.axis_index("ctx") * head_count + lax.axis_index("head")

    def device(i):
        return (i // head_count, i % head_count)

    def load(number, hbm, buf, jj):
        return pltpu.make_async_copy(
            hbm.at[:, pl.ds(jj * wide, wide), :], buf.at[jj], in_sem.at[number, jj]
        )

    def store(jj):
        return pltpu.make_async_copy(
            dq_buf.at[jj], dq_hbm.at[:, pl.ds(jj * wide, wide), :], dq_sem.at[jj]
        )

    def forward(h, jj):
        return pltpu.make_async_remote_copy(
            src_ref=kv_own.at[jj], dst_ref=kv_prev.at[h - 1, jj],
            send_sem=fwd_send.at[h - 1, jj], recv_sem=fwd_recv.at[h - 1, jj],
            device_id=device(me + h), device_id_type=MESH,
        )

    def backward(h, jj):
        return pltpu.make_async_remote_copy(
            src_ref=back_out.at[h - 1, jj], dst_ref=back_in.at[h - 1, jj],
            send_sem=bwd_send.at[h - 1, jj], recv_sem=bwd_recv.at[h - 1, jj],
            device_id=device(me - h), device_id_type=MESH,
        )

    first = [
        pltpu.make_async_copy(k_hbm, kv_raw.at[0], kv_sem.at[0]),
        pltpu.make_async_copy(v_hbm, kv_raw.at[1], kv_sem.at[1]),
        pltpu.make_async_copy(seg_hbm, seg_ref, kv_sem.at[2]),
    ]
    for copy in first:
        copy.start()
    barrier = pltpu.get_barrier_semaphore()
    for h in range(1, halo + 1):
        @pl.when(me >= h)
        def _():
            pl.semaphore_signal(barrier, inc=1, device_id=device(me - h), device_id_type=MESH)

        @pl.when(me + h < devices)
        def _():
            pl.semaphore_signal(barrier, inc=1, device_id=device(me + h), device_id_type=MESH)

    for jj in range(pairs):
        load(0, q_hbm, q_buf, jj).start()
        load(1, g_hbm, g_buf, jj).start()
        load(2, o_hbm, o_buf, jj).start()

    for which in range(2):
        first[which].wait()
        flat[which] = kv_raw[which].astype(jnp.float32).reshape(rows * kv_heads, dim)

    def split(jj):
        for c in range(2):
            for which in range(2):
                kv_own[jj, 2 * c + which] = flat[
                    which, pl.ds(2 * jj + c, rows, stride=kv_heads), :
                ].astype(jnp.bfloat16)

    split(0)
    pl.semaphore_wait(barrier, jnp.minimum(me, halo) + jnp.minimum(devices - 1 - me, halo))

    for jj in range(pairs):
        if jj:
            split(jj)
        for h in range(1, halo + 1):
            @pl.when(me + h < devices)
            def _():
                forward(h, jj).start()

    for h in range(1, halo + 1):
        @pl.when(me < h)
        def _():
            kv_prev[h - 1] = jnp.zeros(kv_prev.shape[1:], kv_prev.dtype)

    first[2].wait()
    token = lax.broadcasted_iota(jnp.int32, (rows, rows * group), 0)
    lane = lax.broadcasted_iota(jnp.int32, (rows, rows * group), 1)
    spread = jnp.where(lane // group == token, 1.0, 0.0).astype(jnp.bfloat16)
    own_seg = seg_ref[pl.ds(me, 1), :].astype(jnp.float32)
    seg_query = nn(jnp.broadcast_to(own_seg, (8, rows)).astype(jnp.bfloat16), spread)[0:1]
    diagonal = lax.broadcasted_iota(jnp.int32, (rows, rows), 0) == lax.broadcasted_iota(
        jnp.int32, (rows, rows), 1
    )
    ones = jnp.ones((rows, lanes), jnp.bfloat16)
    columns = []
    for h in range(halo, -1, -1):
        line = seg_ref[pl.ds(jnp.maximum(me - h, 0), 1), :].astype(jnp.float32)
        line = jnp.where(me >= h, line, -1.0)
        column = jnp.where(diagonal, jnp.broadcast_to(line, (rows, rows)), 0.0)
        columns.append(nn(column.astype(jnp.bfloat16), ones))
    seg_key = jnp.concatenate(columns, axis=0)
    key_row = lax.broadcasted_iota(jnp.int32, (width, lanes), 0)
    query_row = lax.broadcasted_iota(jnp.int32, (width, lanes), 1) // group
    causal = key_row <= query_row + span
    for a in range(parts):
        same = seg_key[a * SUB : a * SUB + width] == seg_query[:, a * lanes : (a + 1) * lanes]
        bias[a] = jnp.where(same & causal, 0.0, MASKED)

    low_half = lax.broadcasted_iota(jnp.int32, (rows * group, dim), 1) < dim // 2

    def pair(jj, _):
        load(0, q_hbm, q_buf, jj).wait()
        load(1, g_hbm, g_buf, jj).wait()
        load(2, o_hbm, o_buf, jj).wait()
        for h in range(1, halo + 1):
            @pl.when(me >= h)
            def _():
                forward(h, jj).wait_recv()

        q_pair = q_buf[jj].astype(jnp.float32)
        g_pair = g_buf[jj].astype(jnp.float32)
        o_pair = o_buf[jj].astype(jnp.float32)
        dq_pair = []
        for c in range(2):
            heads = slice(c * group, (c + 1) * group)
            q = q_pair[:, heads, :].reshape(rows * group, dim).astype(jnp.bfloat16)
            g_wide = g_pair[:, heads, :].reshape(rows * group, dim)
            g = g_wide.astype(jnp.bfloat16)
            product = g_wide * o_pair[:, heads, :].reshape(rows * group, dim)
            product = product + pltpu.roll(product, dim // 2, 1)
            high = product.astype(jnp.bfloat16).astype(jnp.float32)
            terms = jnp.where(low_half, high, product - high).astype(jnp.bfloat16)
            g_terms = jnp.concatenate([g, terms], axis=1)
            k = jnp.concatenate(
                [kv_prev[h - 1, jj, 2 * c] for h in range(halo, 0, -1)] + [kv_own[jj, 2 * c]], axis=0
            )
            v = jnp.concatenate(
                [kv_prev[h - 1, jj, 2 * c + 1] for h in range(halo, 0, -1)] + [kv_own[jj, 2 * c + 1]],
                axis=0,
            )
            v = jnp.concatenate([v, jnp.full(v.shape, -1.0, v.dtype)], axis=1)
            pieces = (span + rows) // SUB
            dk = [None] * pieces
            dv = [None] * pieces
            dq = []
            for a in range(parts):
                q_a = q[a * lanes : (a + 1) * lanes]
                g_a = g[a * lanes : (a + 1) * lanes]
                k_a = k[a * SUB : a * SUB + width]
                v_a = v[a * SUB : a * SUB + width]
                raw = nt(k_a, q_a) + bias[a]
                top = jnp.max(raw, axis=0, keepdims=True)
                e = jnp.exp2((raw - top) * (scale * math.log2(math.e)))
                prob = e * (1.0 / jnp.sum(e, axis=0, keepdims=True))
                d_prob = nt(v_a, g_terms[a * lanes : (a + 1) * lanes])
                d_score = (prob * d_prob).astype(jnp.bfloat16)
                dv_a = nn(prob.astype(jnp.bfloat16), g_a)
                dk_a = nn(d_score, q_a)
                dq.append(tn(d_score, k_a) * scale)
                for b in range(width // SUB):
                    at = slice(b * SUB, (b + 1) * SUB)
                    dk[a + b] = dk_a[at] if dk[a + b] is None else dk[a + b] + dk_a[at]
                    dv[a + b] = dv_a[at] if dv[a + b] is None else dv[a + b] + dv_a[at]
            dq_pair.append(jnp.concatenate(dq, axis=0).reshape(rows, group, dim))
            for h in range(halo, -1, -1):
                at = slice((halo - h) * parts, (halo - h + 1) * parts)
                dk_h = jnp.concatenate(dk[at], axis=0) * scale
                dv_h = jnp.concatenate(dv[at], axis=0)
                if h:
                    back_out[h - 1, jj, 2 * c] = dk_h.astype(jnp.bfloat16)
                    back_out[h - 1, jj, 2 * c + 1] = dv_h.astype(jnp.bfloat16)
                else:
                    own_sum[jj, 2 * c] = dk_h
                    own_sum[jj, 2 * c + 1] = dv_h
        dq_buf[jj] = jnp.concatenate(dq_pair, axis=1).astype(jnp.bfloat16)
        store(jj).start()
        for h in range(1, halo + 1):
            @pl.when(me >= h)
            def _():
                backward(h, jj).start()
        return 0

    lax.fori_loop(0, pairs, pair, 0)

    for jj in range(pairs):
        for h in range(1, halo + 1):
            @pl.when(me + h < devices)
            def _():
                backward(h, jj).wait_recv()
                own_sum[jj] = own_sum[jj] + back_in[h - 1, jj].astype(jnp.float32)
        for c in range(2):
            for which in range(2):
                flat[which, pl.ds(2 * jj + c, rows, stride=kv_heads), :] = own_sum[jj, 2 * c + which]
    last = [
        pltpu.make_async_copy(kv_raw.at[0], dk_hbm, kv_sem.at[0]),
        pltpu.make_async_copy(kv_raw.at[1], dv_hbm, kv_sem.at[1]),
    ]
    for which in range(2):
        kv_raw[which] = flat[which].reshape(rows, kv_heads, dim).astype(jnp.bfloat16)
        last[which].start()

    for jj in range(pairs):
        store(jj).wait()
        for h in range(1, halo + 1):
            @pl.when(me + h < devices)
            def _():
                forward(h, jj).wait_send()

            @pl.when(me >= h)
            def _():
                backward(h, jj).wait_send()
    for copy in last:
        copy.wait()


def write(dq_in, dk_in, dv_in, dq_out, dk_out, dv_out, dq_buf, kv_buf, in_sem, out_sem):
    rows = dq_in.shape[0]
    step = rows // PARTS
    routes = [
        (dq_in.at[pl.ds(c * step, step)], dq_buf.at[pl.ds(c * step, step)], dq_out.at[pl.ds(c * step, step)])
        for c in range(PARTS)
    ]
    routes.append((dk_in, kv_buf.at[0], dk_out))
    routes.append((dv_in, kv_buf.at[1], dv_out))
    loads = [pltpu.make_async_copy(a, b, in_sem.at[n]) for n, (a, b, _) in enumerate(routes)]
    stores = [pltpu.make_async_copy(b, c, out_sem.at[n]) for n, (_, b, c) in enumerate(routes)]
    for copy in loads:
        copy.start()
    for load, store in zip(loads, stores):
        load.wait()
        store.start()
    for copy in stores:
        copy.wait()


def shards(queries, keys, values, outputs, out_grad, segments):
    ctx_count, head_count = lax.axis_size("ctx"), lax.axis_size("head")
    rows, q_heads, dim = queries.shape
    kv_heads = keys.shape[1]
    group = q_heads // kv_heads
    halo = max(1, head_count // 4)
    pairs = kv_heads // 2
    width = halo * rows + SUB
    sizes = (ctx_count, head_count, halo, rows, kv_heads, group, dim)
    lines = segments.reshape(ctx_count * head_count, rows)
    bf16, f32 = jnp.bfloat16, jnp.float32
    big = pltpu.VMEM((pairs, rows, 2 * group, dim), bf16)
    hbm = pl.BlockSpec(memory_space=pl.ANY)
    limit = 56 * 1024 * 1024
    work = rows * q_heads * (halo + 1) * rows
    shapes = (
        jax.ShapeDtypeStruct(queries.shape, bf16),
        jax.ShapeDtypeStruct(keys.shape, bf16),
        jax.ShapeDtypeStruct(values.shape, bf16),
    )
    grads = pl.pallas_call(
        functools.partial(kernel, sizes),
        out_shape=shapes,
        in_specs=[hbm] * 6,
        out_specs=(hbm,) * 3,
        scratch_shapes=[
            big, big, big, big,
            pltpu.VMEM((2, rows, kv_heads, dim), bf16),
            pltpu.VMEM(lines.shape, jnp.int32),
            pltpu.VMEM((2, rows * kv_heads, dim), f32),
            pltpu.VMEM((pairs, 4, rows, dim), bf16),
            pltpu.VMEM((halo, pairs, 4, rows, dim), bf16),
            pltpu.VMEM((halo, pairs, 4, rows, dim), bf16),
            pltpu.VMEM((halo, pairs, 4, rows, dim), bf16),
            pltpu.VMEM((pairs, 4, rows, dim), f32),
            pltpu.VMEM((rows // SUB, width, SUB * group), f32),
            pltpu.SemaphoreType.DMA((3, pairs)),
            pltpu.SemaphoreType.DMA((pairs,)),
            pltpu.SemaphoreType.DMA((3,)),
            pltpu.SemaphoreType.DMA((halo, pairs)),
            pltpu.SemaphoreType.DMA((halo, pairs)),
            pltpu.SemaphoreType.DMA((halo, pairs)),
            pltpu.SemaphoreType.DMA((halo, pairs)),
        ],
        compiler_params=pltpu.CompilerParams(
            collective_id=0, has_side_effects=True, vmem_limit_bytes=limit
        ),
        cost_estimate=pl.CostEstimate(
            flops=10 * work * dim, bytes_accessed=8 * rows * q_heads * dim, transcendentals=work
        ),
    )(queries, keys, values, outputs, out_grad, lines)
    return pl.pallas_call(
        write,
        out_shape=shapes,
        in_specs=[hbm] * 3,
        out_specs=(hbm,) * 3,
        scratch_shapes=[
            pltpu.VMEM(queries.shape, bf16),
            pltpu.VMEM((2, *keys.shape), bf16),
            pltpu.SemaphoreType.DMA((PARTS + 2,)),
            pltpu.SemaphoreType.DMA((PARTS + 2,)),
        ],
        compiler_params=pltpu.CompilerParams(vmem_limit_bytes=limit),
    )(*grads)


def solution(mesh):
    tokens = P(("ctx", "head"), None, None)
    return jax.shard_map(
        shards,
        mesh=mesh,
        in_specs=(tokens, tokens, tokens, tokens, tokens, P()),
        out_specs=(tokens, tokens, tokens),
        check_vma=False,
    )
```

```python
import functools
import math

import jax
import jax.numpy as jnp
from jax import lax
from jax.experimental import pallas as pl
from jax.experimental.pallas import tpu as pltpu
from jax.sharding import PartitionSpec as P

SUB = 32
PARTS = 8
MASKED = -1e30
MESH = pl.DeviceIdType.MESH


def nt(a, b):
    return lax.dot_general(a, b, (((1,), (1,)), ((), ())), preferred_element_type=jnp.float32)


def nn(a, b):
    return jnp.dot(a, b, preferred_element_type=jnp.float32)


def tn(a, b):
    return lax.dot_general(a, b, (((0,), (0,)), ((), ())), preferred_element_type=jnp.float32)


def kernel(
    sizes,
    q_hbm, k_hbm, v_hbm, o_hbm, g_hbm, seg_hbm,
    dq_hbm, dk_hbm, dv_hbm,
    q_buf, g_buf, o_buf, dq_buf, q_rows, g_rows, kv_raw, seg_ref, flat, kv_own, kv_prev, back_out, back_in, own_sum, bias,
    in_sem, dq_sem, kv_sem, fwd_send, fwd_recv, bwd_send, bwd_recv,
):
    ctx_count, head_count, halo, rows, kv_heads, group, dim = sizes
    devices = ctx_count * head_count
    span = halo * rows
    pairs = kv_heads // 2
    wide = 2 * group
    lanes = SUB * group
    width = span + SUB
    parts = rows // SUB
    scale = dim ** (-0.5)
    me = lax.axis_index("ctx") * head_count + lax.axis_index("head")

    def device(i):
        return (i // head_count, i % head_count)

    def load(number, hbm, buf, jj):
        return pltpu.make_async_copy(
            hbm.at[:, pl.ds(jj * wide, wide), :], buf.at[jj], in_sem.at[number, jj]
        )

    def store(jj):
        return pltpu.make_async_copy(
            dq_buf.at[jj], dq_hbm.at[:, pl.ds(jj * wide, wide), :], dq_sem.at[jj]
        )

    def forward(h, jj):
        return pltpu.make_async_remote_copy(
            src_ref=kv_own.at[jj], dst_ref=kv_prev.at[h - 1, jj],
            send_sem=fwd_send.at[h - 1, jj], recv_sem=fwd_recv.at[h - 1, jj],
            device_id=device(me + h), device_id_type=MESH,
        )

    def backward(h, jj):
        return pltpu.make_async_remote_copy(
            src_ref=back_out.at[h - 1, jj], dst_ref=back_in.at[h - 1, jj],
            send_sem=bwd_send.at[h - 1, jj], recv_sem=bwd_recv.at[h - 1, jj],
            device_id=device(me - h), device_id_type=MESH,
        )

    first = [
        pltpu.make_async_copy(k_hbm, kv_raw.at[0], kv_sem.at[0]),
        pltpu.make_async_copy(v_hbm, kv_raw.at[1], kv_sem.at[1]),
        pltpu.make_async_copy(seg_hbm, seg_ref, kv_sem.at[2]),
    ]
    for copy in first:
        copy.start()
    barrier = pltpu.get_barrier_semaphore()
    for h in range(1, halo + 1):
        @pl.when(me >= h)
        def _():
            pl.semaphore_signal(barrier, inc=1, device_id=device(me - h), device_id_type=MESH)

        @pl.when(me + h < devices)
        def _():
            pl.semaphore_signal(barrier, inc=1, device_id=device(me + h), device_id_type=MESH)

    for jj in range(pairs):
        load(0, q_hbm, q_buf, jj).start()
        load(1, g_hbm, g_buf, jj).start()
        load(2, o_hbm, o_buf, jj).start()

    for which in range(2):
        first[which].wait()
        flat[which] = kv_raw[which].astype(jnp.float32).reshape(rows * kv_heads, dim)

    def split(jj):
        for c in range(2):
            for which in range(2):
                kv_own[jj, 2 * c + which] = flat[
                    which, pl.ds(2 * jj + c, rows, stride=kv_heads), :
                ].astype(jnp.bfloat16)

    split(0)
    pl.semaphore_wait(barrier, jnp.minimum(me, halo) + jnp.minimum(devices - 1 - me, halo))

    for jj in range(pairs):
        if jj:
            split(jj)
        for h in range(1, halo + 1):
            @pl.when(me + h < devices)
            def _():
                forward(h, jj).start()

    for h in range(1, halo + 1):
        @pl.when(me < h)
        def _():
            kv_prev[h - 1] = jnp.zeros(kv_prev.shape[1:], kv_prev.dtype)

    first[2].wait()
    token = lax.broadcasted_iota(jnp.int32, (rows, rows * group), 0)
    lane = lax.broadcasted_iota(jnp.int32, (rows, rows * group), 1)
    spread = jnp.where(lane // group == token, 1.0, 0.0).astype(jnp.bfloat16)
    own_seg = seg_ref[pl.ds(me, 1), :].astype(jnp.float32)
    seg_query = nn(jnp.broadcast_to(own_seg, (8, rows)).astype(jnp.bfloat16), spread)[0:1]
    diagonal = lax.broadcasted_iota(jnp.int32, (rows, rows), 0) == lax.broadcasted_iota(
        jnp.int32, (rows, rows), 1
    )
    ones = jnp.ones((rows, lanes), jnp.bfloat16)
    columns = []
    for h in range(halo, -1, -1):
        line = seg_ref[pl.ds(jnp.maximum(me - h, 0), 1), :].astype(jnp.float32)
        line = jnp.where(me >= h, line, -1.0)
        column = jnp.where(diagonal, jnp.broadcast_to(line, (rows, rows)), 0.0)
        columns.append(nn(column.astype(jnp.bfloat16), ones))
    seg_key = jnp.concatenate(columns, axis=0)
    key_row = lax.broadcasted_iota(jnp.int32, (width, lanes), 0)
    query_row = lax.broadcasted_iota(jnp.int32, (width, lanes), 1) // group
    causal = key_row <= query_row + span
    for a in range(parts):
        same = seg_key[a * SUB : a * SUB + width] == seg_query[:, a * lanes : (a + 1) * lanes]
        bias[a] = jnp.where(same & causal, 0.0, MASKED)

    low_half = lax.broadcasted_iota(jnp.int32, (rows * group, dim), 1) < dim // 2

    def prepare(jj, _):
        load(0, q_hbm, q_buf, jj).wait()
        load(1, g_hbm, g_buf, jj).wait()
        load(2, o_hbm, o_buf, jj).wait()
        q_pair = q_buf[jj].astype(jnp.float32)
        g_pair = g_buf[jj].astype(jnp.float32)
        o_pair = o_buf[jj].astype(jnp.float32)
        for c in range(2):
            heads = slice(c * group, (c + 1) * group)
            q_wide = q_pair[:, heads, :].reshape(rows * group, dim)
            g_wide = g_pair[:, heads, :].reshape(rows * group, dim)
            product = g_wide * o_pair[:, heads, :].reshape(rows * group, dim)
            product = product + pltpu.roll(product, dim // 2, 1)
            high = product.astype(jnp.bfloat16).astype(jnp.float32)
            terms = jnp.where(low_half, high, product - high)
            q_rows[2 * jj + c] = q_wide.astype(jnp.bfloat16)
            g_rows[2 * jj + c, :, :dim] = g_wide.astype(jnp.bfloat16)
            g_rows[2 * jj + c, :, dim:] = terms.astype(jnp.bfloat16)
        return 0

    lax.fori_loop(0, pairs, prepare, 0)

    def pair(jj, _):
        for h in range(1, halo + 1):
            @pl.when(me >= h)
            def _():
                forward(h, jj).wait_recv()

        dq_pair = []
        for c in range(2):
            q = q_rows[2 * jj + c]
            g_terms = g_rows[2 * jj + c]
            g = g_terms[:, :dim]
            k = jnp.concatenate(
                [kv_prev[h - 1, jj, 2 * c] for h in range(halo, 0, -1)] + [kv_own[jj, 2 * c]], axis=0
            )
            v = jnp.concatenate(
                [kv_prev[h - 1, jj, 2 * c + 1] for h in range(halo, 0, -1)] + [kv_own[jj, 2 * c + 1]],
                axis=0,
            )
            v = jnp.concatenate([v, jnp.full(v.shape, -1.0, v.dtype)], axis=1)
            pieces = (span + rows) // SUB
            dk = [None] * pieces
            dv = [None] * pieces
            dq = []
            for a in range(parts):
                q_a = q[a * lanes : (a + 1) * lanes]
                g_a = g[a * lanes : (a + 1) * lanes]
                k_a = k[a * SUB : a * SUB + width]
                v_a = v[a * SUB : a * SUB + width]
                raw = nt(k_a, q_a) + bias[a]
                top = jnp.max(raw, axis=0, keepdims=True)
                e = jnp.exp2((raw - top) * (scale * math.log2(math.e)))
                prob = e * (1.0 / jnp.sum(e, axis=0, keepdims=True))
                d_prob = nt(v_a, g_terms[a * lanes : (a + 1) * lanes])
                d_score = (prob * d_prob).astype(jnp.bfloat16)
                dv_a = nn(prob.astype(jnp.bfloat16), g_a)
                dk_a = nn(d_score, q_a)
                dq.append(tn(d_score, k_a) * scale)
                for b in range(width // SUB):
                    at = slice(b * SUB, (b + 1) * SUB)
                    dk[a + b] = dk_a[at] if dk[a + b] is None else dk[a + b] + dk_a[at]
                    dv[a + b] = dv_a[at] if dv[a + b] is None else dv[a + b] + dv_a[at]
            dq_pair.append(jnp.concatenate(dq, axis=0).reshape(rows, group, dim))
            for h in range(halo, -1, -1):
                at = slice((halo - h) * parts, (halo - h + 1) * parts)
                dk_h = jnp.concatenate(dk[at], axis=0) * scale
                dv_h = jnp.concatenate(dv[at], axis=0)
                if h:
                    back_out[h - 1, jj, 2 * c] = dk_h.astype(jnp.bfloat16)
                    back_out[h - 1, jj, 2 * c + 1] = dv_h.astype(jnp.bfloat16)
                else:
                    own_sum[jj, 2 * c] = dk_h
                    own_sum[jj, 2 * c + 1] = dv_h
        dq_buf[jj] = jnp.concatenate(dq_pair, axis=1).astype(jnp.bfloat16)
        store(jj).start()
        for h in range(1, halo + 1):
            @pl.when(me >= h)
            def _():
                backward(h, jj).start()
        return 0

    lax.fori_loop(0, pairs, pair, 0)

    for jj in range(pairs):
        for h in range(1, halo + 1):
            @pl.when(me + h < devices)
            def _():
                backward(h, jj).wait_recv()
                own_sum[jj] = own_sum[jj] + back_in[h - 1, jj].astype(jnp.float32)
        for c in range(2):
            for which in range(2):
                flat[which, pl.ds(2 * jj + c, rows, stride=kv_heads), :] = own_sum[jj, 2 * c + which]
    last = [
        pltpu.make_async_copy(kv_raw.at[0], dk_hbm, kv_sem.at[0]),
        pltpu.make_async_copy(kv_raw.at[1], dv_hbm, kv_sem.at[1]),
    ]
    for which in range(2):
        kv_raw[which] = flat[which].reshape(rows, kv_heads, dim).astype(jnp.bfloat16)
        last[which].start()

    for jj in range(pairs):
        store(jj).wait()
        for h in range(1, halo + 1):
            @pl.when(me + h < devices)
            def _():
                forward(h, jj).wait_send()

            @pl.when(me >= h)
            def _():
                backward(h, jj).wait_send()
    for copy in last:
        copy.wait()


def write(dq_in, dk_in, dv_in, dq_out, dk_out, dv_out, dq_buf, kv_buf, in_sem, out_sem):
    rows = dq_in.shape[0]
    step = rows // PARTS
    routes = [
        (dq_in.at[pl.ds(c * step, step)], dq_buf.at[pl.ds(c * step, step)], dq_out.at[pl.ds(c * step, step)])
        for c in range(PARTS)
    ]
    routes.append((dk_in, kv_buf.at[0], dk_out))
    routes.append((dv_in, kv_buf.at[1], dv_out))
    loads = [pltpu.make_async_copy(a, b, in_sem.at[n]) for n, (a, b, _) in enumerate(routes)]
    stores = [pltpu.make_async_copy(b, c, out_sem.at[n]) for n, (_, b, c) in enumerate(routes)]
    for copy in loads:
        copy.start()
    for load, store in zip(loads, stores):
        load.wait()
        store.start()
    for copy in stores:
        copy.wait()


def shards(queries, keys, values, outputs, out_grad, segments):
    ctx_count, head_count = lax.axis_size("ctx"), lax.axis_size("head")
    rows, q_heads, dim = queries.shape
    kv_heads = keys.shape[1]
    group = q_heads // kv_heads
    halo = max(1, head_count // 4)
    pairs = kv_heads // 2
    width = halo * rows + SUB
    sizes = (ctx_count, head_count, halo, rows, kv_heads, group, dim)
    lines = segments.reshape(ctx_count * head_count, rows)
    bf16, f32 = jnp.bfloat16, jnp.float32
    big = pltpu.VMEM((pairs, rows, 2 * group, dim), bf16)
    hbm = pl.BlockSpec(memory_space=pl.ANY)
    limit = 56 * 1024 * 1024
    work = rows * q_heads * (halo + 1) * rows
    shapes = (
        jax.ShapeDtypeStruct(queries.shape, bf16),
        jax.ShapeDtypeStruct(keys.shape, bf16),
        jax.ShapeDtypeStruct(values.shape, bf16),
    )
    grads = pl.pallas_call(
        functools.partial(kernel, sizes),
        out_shape=shapes,
        in_specs=[hbm] * 6,
        out_specs=(hbm,) * 3,
        scratch_shapes=[
            big, big, big, big,
            pltpu.VMEM((kv_heads, rows * group, dim), bf16),
            pltpu.VMEM((kv_heads, rows * group, 2 * dim), bf16),
            pltpu.VMEM((2, rows, kv_heads, dim), bf16),
            pltpu.VMEM(lines.shape, jnp.int32),
            pltpu.VMEM((2, rows * kv_heads, dim), f32),
            pltpu.VMEM((pairs, 4, rows, dim), bf16),
            pltpu.VMEM((halo, pairs, 4, rows, dim), bf16),
            pltpu.VMEM((halo, pairs, 4, rows, dim), bf16),
            pltpu.VMEM((halo, pairs, 4, rows, dim), bf16),
            pltpu.VMEM((pairs, 4, rows, dim), f32),
            pltpu.VMEM((rows // SUB, width, SUB * group), f32),
            pltpu.SemaphoreType.DMA((3, pairs)),
            pltpu.SemaphoreType.DMA((pairs,)),
            pltpu.SemaphoreType.DMA((3,)),
            pltpu.SemaphoreType.DMA((halo, pairs)),
            pltpu.SemaphoreType.DMA((halo, pairs)),
            pltpu.SemaphoreType.DMA((halo, pairs)),
            pltpu.SemaphoreType.DMA((halo, pairs)),
        ],
        compiler_params=pltpu.CompilerParams(
            collective_id=0, has_side_effects=True, vmem_limit_bytes=limit
        ),
        cost_estimate=pl.CostEstimate(
            flops=10 * work * dim, bytes_accessed=8 * rows * q_heads * dim, transcendentals=work
        ),
    )(queries, keys, values, outputs, out_grad, lines)
    return pl.pallas_call(
        write,
        out_shape=shapes,
        in_specs=[hbm] * 3,
        out_specs=(hbm,) * 3,
        scratch_shapes=[
            pltpu.VMEM(queries.shape, bf16),
            pltpu.VMEM((2, *keys.shape), bf16),
            pltpu.SemaphoreType.DMA((PARTS + 2,)),
            pltpu.SemaphoreType.DMA((PARTS + 2,)),
        ],
        compiler_params=pltpu.CompilerParams(vmem_limit_bytes=limit),
    )(*grads)


def solution(mesh):
    tokens = P(("ctx", "head"), None, None)
    return jax.shard_map(
        shards,
        mesh=mesh,
        in_specs=(tokens, tokens, tokens, tokens, tokens, P()),
        out_specs=(tokens, tokens, tokens),
        check_vma=False,
    )
```

```python
import functools
import math

import jax
import jax.numpy as jnp
from jax import lax
from jax.experimental import pallas as pl
from jax.experimental.pallas import tpu as pltpu
from jax.sharding import PartitionSpec as P

SUB = 32
PARTS = 8
MASKED = -1e30
MESH = pl.DeviceIdType.MESH


def nt(a, b):
    return lax.dot_general(a, b, (((1,), (1,)), ((), ())), preferred_element_type=jnp.float32)


def nn(a, b):
    return jnp.dot(a, b, preferred_element_type=jnp.float32)


def tn(a, b):
    return lax.dot_general(a, b, (((0,), (0,)), ((), ())), preferred_element_type=jnp.float32)


def kernel(
    sizes,
    q_hbm, k_hbm, v_hbm, o_hbm, g_hbm, seg_hbm,
    dq_hbm, dk_hbm, dv_hbm,
    q_buf, g_buf, o_buf, dq_buf, q_rows, g_rows, kv_raw, seg_ref, flat, kv_own, kv_prev, back_out, back_in, own_sum, bias,
    in_sem, dq_sem, kv_sem, fwd_send, fwd_recv, bwd_send, bwd_recv,
):
    ctx_count, head_count, halo, rows, kv_heads, group, dim = sizes
    devices = ctx_count * head_count
    span = halo * rows
    pairs = kv_heads // 2
    wide = 2 * group
    lanes = SUB * group
    width = span + SUB
    parts = rows // SUB
    scale = dim ** (-0.5)
    me = lax.axis_index("ctx") * head_count + lax.axis_index("head")

    def device(i):
        return (i // head_count, i % head_count)

    def load(number, hbm, buf, jj):
        return pltpu.make_async_copy(
            hbm.at[:, pl.ds(jj * wide, wide), :], buf.at[jj], in_sem.at[number, jj]
        )

    def store(jj):
        return pltpu.make_async_copy(
            dq_buf.at[jj], dq_hbm.at[:, pl.ds(jj * wide, wide), :], dq_sem.at[jj]
        )

    def forward(h, j):
        return pltpu.make_async_remote_copy(
            src_ref=kv_own.at[j], dst_ref=kv_prev.at[h - 1, j],
            send_sem=fwd_send.at[h - 1, j], recv_sem=fwd_recv.at[h - 1, j],
            device_id=device(me + h), device_id_type=MESH,
        )

    def backward(h, j):
        return pltpu.make_async_remote_copy(
            src_ref=back_out.at[h - 1, j], dst_ref=back_in.at[h - 1, j],
            send_sem=bwd_send.at[h - 1, j], recv_sem=bwd_recv.at[h - 1, j],
            device_id=device(me - h), device_id_type=MESH,
        )

    first = [
        pltpu.make_async_copy(k_hbm, kv_raw.at[0], kv_sem.at[0]),
        pltpu.make_async_copy(v_hbm, kv_raw.at[1], kv_sem.at[1]),
        pltpu.make_async_copy(seg_hbm, seg_ref, kv_sem.at[2]),
    ]
    for copy in first:
        copy.start()
    barrier = pltpu.get_barrier_semaphore()
    for h in range(1, halo + 1):
        @pl.when(me >= h)
        def _():
            pl.semaphore_signal(barrier, inc=1, device_id=device(me - h), device_id_type=MESH)

        @pl.when(me + h < devices)
        def _():
            pl.semaphore_signal(barrier, inc=1, device_id=device(me + h), device_id_type=MESH)

    for jj in range(pairs):
        load(0, q_hbm, q_buf, jj).start()
        load(1, g_hbm, g_buf, jj).start()
        load(2, o_hbm, o_buf, jj).start()

    for which in range(2):
        first[which].wait()
        flat[which] = kv_raw[which].astype(jnp.float32).reshape(rows * kv_heads, dim)

    def split(j):
        for which in range(2):
            kv_own[j, which] = flat[which, pl.ds(j, rows, stride=kv_heads), :].astype(jnp.bfloat16)

    split(0)
    pl.semaphore_wait(barrier, jnp.minimum(me, halo) + jnp.minimum(devices - 1 - me, halo))

    for j in range(kv_heads):
        if j:
            split(j)
        for h in range(1, halo + 1):
            @pl.when(me + h < devices)
            def _():
                forward(h, j).start()

    for h in range(1, halo + 1):
        @pl.when(me < h)
        def _():
            kv_prev[h - 1] = jnp.zeros(kv_prev.shape[1:], kv_prev.dtype)

    first[2].wait()
    token = lax.broadcasted_iota(jnp.int32, (rows, rows * group), 0)
    lane = lax.broadcasted_iota(jnp.int32, (rows, rows * group), 1)
    spread = jnp.where(lane // group == token, 1.0, 0.0).astype(jnp.bfloat16)
    own_seg = seg_ref[pl.ds(me, 1), :].astype(jnp.float32)
    seg_query = nn(jnp.broadcast_to(own_seg, (8, rows)).astype(jnp.bfloat16), spread)[0:1]
    diagonal = lax.broadcasted_iota(jnp.int32, (rows, rows), 0) == lax.broadcasted_iota(
        jnp.int32, (rows, rows), 1
    )
    ones = jnp.ones((rows, lanes), jnp.bfloat16)
    columns = []
    for h in range(halo, -1, -1):
        line = seg_ref[pl.ds(jnp.maximum(me - h, 0), 1), :].astype(jnp.float32)
        line = jnp.where(me >= h, line, -1.0)
        column = jnp.where(diagonal, jnp.broadcast_to(line, (rows, rows)), 0.0)
        columns.append(nn(column.astype(jnp.bfloat16), ones))
    seg_key = jnp.concatenate(columns, axis=0)
    key_row = lax.broadcasted_iota(jnp.int32, (width, lanes), 0)
    query_row = lax.broadcasted_iota(jnp.int32, (width, lanes), 1) // group
    causal = key_row <= query_row + span
    for a in range(parts):
        same = seg_key[a * SUB : a * SUB + width] == seg_query[:, a * lanes : (a + 1) * lanes]
        bias[a] = jnp.where(same & causal, 0.0, MASKED)

    low_half = lax.broadcasted_iota(jnp.int32, (rows * group, dim), 1) < dim // 2

    def prepare(jj, _):
        load(0, q_hbm, q_buf, jj).wait()
        load(1, g_hbm, g_buf, jj).wait()
        load(2, o_hbm, o_buf, jj).wait()
        q_pair = q_buf[jj].astype(jnp.float32)
        g_pair = g_buf[jj].astype(jnp.float32)
        o_pair = o_buf[jj].astype(jnp.float32)
        for c in range(2):
            heads = slice(c * group, (c + 1) * group)
            q_wide = q_pair[:, heads, :].reshape(rows * group, dim)
            g_wide = g_pair[:, heads, :].reshape(rows * group, dim)
            product = g_wide * o_pair[:, heads, :].reshape(rows * group, dim)
            product = product + pltpu.roll(product, dim // 2, 1)
            high = product.astype(jnp.bfloat16).astype(jnp.float32)
            terms = jnp.where(low_half, high, product - high)
            q_rows[2 * jj + c] = q_wide.astype(jnp.bfloat16)
            g_rows[2 * jj + c, :, :dim] = g_wide.astype(jnp.bfloat16)
            g_rows[2 * jj + c, :, dim:] = terms.astype(jnp.bfloat16)
        return 0

    lax.fori_loop(0, pairs, prepare, 0)

    def pair(jj, _):
        dq_pair = []
        for c in range(2):
            j = 2 * jj + c
            for h in range(1, halo + 1):
                @pl.when(me >= h)
                def _():
                    forward(h, j).wait_recv()

            q = q_rows[j]
            g_terms = g_rows[j]
            g = g_terms[:, :dim]
            k = jnp.concatenate([kv_prev[h - 1, j, 0] for h in range(halo, 0, -1)] + [kv_own[j, 0]], axis=0)
            v = jnp.concatenate([kv_prev[h - 1, j, 1] for h in range(halo, 0, -1)] + [kv_own[j, 1]], axis=0)
            v = jnp.concatenate([v, jnp.full(v.shape, -1.0, v.dtype)], axis=1)
            pieces = (span + rows) // SUB
            dk = [None] * pieces
            dv = [None] * pieces
            dq = []
            for a in range(parts):
                q_a = q[a * lanes : (a + 1) * lanes]
                g_a = g[a * lanes : (a + 1) * lanes]
                k_a = k[a * SUB : a * SUB + width]
                v_a = v[a * SUB : a * SUB + width]
                raw = nt(k_a, q_a) + bias[a]
                top = jnp.max(raw, axis=0, keepdims=True)
                e = jnp.exp2((raw - top) * (scale * math.log2(math.e)))
                prob = e * (1.0 / jnp.sum(e, axis=0, keepdims=True))
                d_prob = nt(v_a, g_terms[a * lanes : (a + 1) * lanes])
                d_score = (prob * d_prob).astype(jnp.bfloat16)
                dv_a = nn(prob.astype(jnp.bfloat16), g_a)
                dk_a = nn(d_score, q_a)
                dq.append(tn(d_score, k_a) * scale)
                for b in range(width // SUB):
                    at = slice(b * SUB, (b + 1) * SUB)
                    dk[a + b] = dk_a[at] if dk[a + b] is None else dk[a + b] + dk_a[at]
                    dv[a + b] = dv_a[at] if dv[a + b] is None else dv[a + b] + dv_a[at]
            dq_pair.append(jnp.concatenate(dq, axis=0).reshape(rows, group, dim))
            for h in range(halo, -1, -1):
                at = slice((halo - h) * parts, (halo - h + 1) * parts)
                dk_h = jnp.concatenate(dk[at], axis=0) * scale
                dv_h = jnp.concatenate(dv[at], axis=0)
                if h:
                    back_out[h - 1, j, 0] = dk_h.astype(jnp.bfloat16)
                    back_out[h - 1, j, 1] = dv_h.astype(jnp.bfloat16)
                else:
                    own_sum[j, 0] = dk_h
                    own_sum[j, 1] = dv_h
            for h in range(1, halo + 1):
                @pl.when(me >= h)
                def _():
                    backward(h, j).start()
        dq_buf[jj] = jnp.concatenate(dq_pair, axis=1).astype(jnp.bfloat16)
        store(jj).start()
        return 0

    lax.fori_loop(0, pairs, pair, 0)

    for j in range(kv_heads):
        for h in range(1, halo + 1):
            @pl.when(me + h < devices)
            def _():
                backward(h, j).wait_recv()
                own_sum[j] = own_sum[j] + back_in[h - 1, j].astype(jnp.float32)
        for which in range(2):
            flat[which, pl.ds(j, rows, stride=kv_heads), :] = own_sum[j, which]
    last = [
        pltpu.make_async_copy(kv_raw.at[0], dk_hbm, kv_sem.at[0]),
        pltpu.make_async_copy(kv_raw.at[1], dv_hbm, kv_sem.at[1]),
    ]
    for which in range(2):
        kv_raw[which] = flat[which].reshape(rows, kv_heads, dim).astype(jnp.bfloat16)
        last[which].start()

    for jj in range(pairs):
        store(jj).wait()
    for j in range(kv_heads):
        for h in range(1, halo + 1):
            @pl.when(me + h < devices)
            def _():
                forward(h, j).wait_send()

            @pl.when(me >= h)
            def _():
                backward(h, j).wait_send()
    for copy in last:
        copy.wait()


def write(dq_in, dk_in, dv_in, dq_out, dk_out, dv_out, dq_buf, kv_buf, in_sem, out_sem):
    rows = dq_in.shape[0]
    step = rows // PARTS
    routes = [
        (dq_in.at[pl.ds(c * step, step)], dq_buf.at[pl.ds(c * step, step)], dq_out.at[pl.ds(c * step, step)])
        for c in range(PARTS)
    ]
    routes.append((dk_in, kv_buf.at[0], dk_out))
    routes.append((dv_in, kv_buf.at[1], dv_out))
    loads = [pltpu.make_async_copy(a, b, in_sem.at[n]) for n, (a, b, _) in enumerate(routes)]
    stores = [pltpu.make_async_copy(b, c, out_sem.at[n]) for n, (_, b, c) in enumerate(routes)]
    for copy in loads:
        copy.start()
    for load, store in zip(loads, stores):
        load.wait()
        store.start()
    for copy in stores:
        copy.wait()


def shards(queries, keys, values, outputs, out_grad, segments):
    ctx_count, head_count = lax.axis_size("ctx"), lax.axis_size("head")
    rows, q_heads, dim = queries.shape
    kv_heads = keys.shape[1]
    group = q_heads // kv_heads
    halo = max(1, head_count // 4)
    pairs = kv_heads // 2
    width = halo * rows + SUB
    sizes = (ctx_count, head_count, halo, rows, kv_heads, group, dim)
    lines = segments.reshape(ctx_count * head_count, rows)
    bf16, f32 = jnp.bfloat16, jnp.float32
    big = pltpu.VMEM((pairs, rows, 2 * group, dim), bf16)
    hbm = pl.BlockSpec(memory_space=pl.ANY)
    limit = 56 * 1024 * 1024
    work = rows * q_heads * (halo + 1) * rows
    shapes = (
        jax.ShapeDtypeStruct(queries.shape, bf16),
        jax.ShapeDtypeStruct(keys.shape, bf16),
        jax.ShapeDtypeStruct(values.shape, bf16),
    )
    grads = pl.pallas_call(
        functools.partial(kernel, sizes),
        out_shape=shapes,
        in_specs=[hbm] * 6,
        out_specs=(hbm,) * 3,
        scratch_shapes=[
            big, big, big, big,
            pltpu.VMEM((kv_heads, rows * group, dim), bf16),
            pltpu.VMEM((kv_heads, rows * group, 2 * dim), bf16),
            pltpu.VMEM((2, rows, kv_heads, dim), bf16),
            pltpu.VMEM(lines.shape, jnp.int32),
            pltpu.VMEM((2, rows * kv_heads, dim), f32),
            pltpu.VMEM((kv_heads, 2, rows, dim), bf16),
            pltpu.VMEM((halo, kv_heads, 2, rows, dim), bf16),
            pltpu.VMEM((halo, kv_heads, 2, rows, dim), bf16),
            pltpu.VMEM((halo, kv_heads, 2, rows, dim), bf16),
            pltpu.VMEM((kv_heads, 2, rows, dim), f32),
            pltpu.VMEM((rows // SUB, width, SUB * group), f32),
            pltpu.SemaphoreType.DMA((3, pairs)),
            pltpu.SemaphoreType.DMA((pairs,)),
            pltpu.SemaphoreType.DMA((3,)),
            pltpu.SemaphoreType.DMA((halo, kv_heads)),
            pltpu.SemaphoreType.DMA((halo, kv_heads)),
            pltpu.SemaphoreType.DMA((halo, kv_heads)),
            pltpu.SemaphoreType.DMA((halo, kv_heads)),
        ],
        compiler_params=pltpu.CompilerParams(
            collective_id=0, has_side_effects=True, vmem_limit_bytes=limit
        ),
        cost_estimate=pl.CostEstimate(
            flops=10 * work * dim, bytes_accessed=8 * rows * q_heads * dim, transcendentals=work
        ),
    )(queries, keys, values, outputs, out_grad, lines)
    return pl.pallas_call(
        write,
        out_shape=shapes,
        in_specs=[hbm] * 3,
        out_specs=(hbm,) * 3,
        scratch_shapes=[
            pltpu.VMEM(queries.shape, bf16),
            pltpu.VMEM((2, *keys.shape), bf16),
            pltpu.SemaphoreType.DMA((PARTS + 2,)),
            pltpu.SemaphoreType.DMA((PARTS + 2,)),
        ],
        compiler_params=pltpu.CompilerParams(vmem_limit_bytes=limit),
    )(*grads)


def solution(mesh):
    tokens = P(("ctx", "head"), None, None)
    return jax.shard_map(
        shards,
        mesh=mesh,
        in_specs=(tokens, tokens, tokens, tokens, tokens, P()),
        out_specs=(tokens, tokens, tokens),
        check_vma=False,
    )
```

```python
import functools
import math

import jax
import jax.numpy as jnp
from jax import lax
from jax.experimental import pallas as pl
from jax.experimental.pallas import tpu as pltpu
from jax.sharding import PartitionSpec as P

SUB = 64
PARTS = 8
MASKED = -1e30
MESH = pl.DeviceIdType.MESH


def nt(a, b):
    return lax.dot_general(a, b, (((1,), (1,)), ((), ())), preferred_element_type=jnp.float32)


def nn(a, b):
    return jnp.dot(a, b, preferred_element_type=jnp.float32)


def tn(a, b):
    return lax.dot_general(a, b, (((0,), (0,)), ((), ())), preferred_element_type=jnp.float32)


def kernel(
    sizes,
    q_hbm, k_hbm, v_hbm, o_hbm, g_hbm, seg_hbm,
    dq_hbm, dk_hbm, dv_hbm,
    q_buf, g_buf, o_buf, dq_buf, q_rows, g_rows, kv_raw, seg_ref, flat, kv_own, kv_prev, back_out, back_in, own_sum, bias,
    in_sem, dq_sem, kv_sem, fwd_send, fwd_recv, bwd_send, bwd_recv,
):
    ctx_count, head_count, halo, rows, kv_heads, group, dim = sizes
    devices = ctx_count * head_count
    span = halo * rows
    pairs = kv_heads // 2
    wide = 2 * group
    lanes = SUB * group
    width = span + SUB
    parts = rows // SUB
    scale = dim ** (-0.5)
    me = lax.axis_index("ctx") * head_count + lax.axis_index("head")

    def device(i):
        return (i // head_count, i % head_count)

    def load(number, hbm, buf, jj):
        return pltpu.make_async_copy(
            hbm.at[:, pl.ds(jj * wide, wide), :], buf.at[jj], in_sem.at[number, jj]
        )

    def store(jj):
        return pltpu.make_async_copy(
            dq_buf.at[jj], dq_hbm.at[:, pl.ds(jj * wide, wide), :], dq_sem.at[jj]
        )

    def forward(h, j):
        return pltpu.make_async_remote_copy(
            src_ref=kv_own.at[j], dst_ref=kv_prev.at[h - 1, j],
            send_sem=fwd_send.at[h - 1, j], recv_sem=fwd_recv.at[h - 1, j],
            device_id=device(me + h), device_id_type=MESH,
        )

    def backward(h, j):
        return pltpu.make_async_remote_copy(
            src_ref=back_out.at[h - 1, j], dst_ref=back_in.at[h - 1, j],
            send_sem=bwd_send.at[h - 1, j], recv_sem=bwd_recv.at[h - 1, j],
            device_id=device(me - h), device_id_type=MESH,
        )

    first = [
        pltpu.make_async_copy(k_hbm, kv_raw.at[0], kv_sem.at[0]),
        pltpu.make_async_copy(v_hbm, kv_raw.at[1], kv_sem.at[1]),
        pltpu.make_async_copy(seg_hbm, seg_ref, kv_sem.at[2]),
    ]
    for copy in first:
        copy.start()
    barrier = pltpu.get_barrier_semaphore()
    for h in range(1, halo + 1):
        @pl.when(me >= h)
        def _():
            pl.semaphore_signal(barrier, inc=1, device_id=device(me - h), device_id_type=MESH)

        @pl.when(me + h < devices)
        def _():
            pl.semaphore_signal(barrier, inc=1, device_id=device(me + h), device_id_type=MESH)

    for jj in range(pairs):
        load(0, q_hbm, q_buf, jj).start()
        load(1, g_hbm, g_buf, jj).start()
        load(2, o_hbm, o_buf, jj).start()

    for which in range(2):
        first[which].wait()
        flat[which] = kv_raw[which].astype(jnp.float32).reshape(rows * kv_heads, dim)

    def split(j):
        for which in range(2):
            kv_own[j, which] = flat[which, pl.ds(j, rows, stride=kv_heads), :].astype(jnp.bfloat16)

    split(0)
    pl.semaphore_wait(barrier, jnp.minimum(me, halo) + jnp.minimum(devices - 1 - me, halo))

    for j in range(kv_heads):
        if j:
            split(j)
        for h in range(1, halo + 1):
            @pl.when(me + h < devices)
            def _():
                forward(h, j).start()

    for h in range(1, halo + 1):
        @pl.when(me < h)
        def _():
            kv_prev[h - 1] = jnp.zeros(kv_prev.shape[1:], kv_prev.dtype)

    first[2].wait()
    token = lax.broadcasted_iota(jnp.int32, (rows, rows * group), 0)
    lane = lax.broadcasted_iota(jnp.int32, (rows, rows * group), 1)
    spread = jnp.where(lane // group == token, 1.0, 0.0).astype(jnp.bfloat16)
    own_seg = seg_ref[pl.ds(me, 1), :].astype(jnp.float32)
    seg_query = nn(jnp.broadcast_to(own_seg, (8, rows)).astype(jnp.bfloat16), spread)[0:1]
    diagonal = lax.broadcasted_iota(jnp.int32, (rows, rows), 0) == lax.broadcasted_iota(
        jnp.int32, (rows, rows), 1
    )
    ones = jnp.ones((rows, lanes), jnp.bfloat16)
    columns = []
    for h in range(halo, -1, -1):
        line = seg_ref[pl.ds(jnp.maximum(me - h, 0), 1), :].astype(jnp.float32)
        line = jnp.where(me >= h, line, -1.0)
        column = jnp.where(diagonal, jnp.broadcast_to(line, (rows, rows)), 0.0)
        columns.append(nn(column.astype(jnp.bfloat16), ones))
    seg_key = jnp.concatenate(columns, axis=0)
    key_row = lax.broadcasted_iota(jnp.int32, (width, lanes), 0)
    query_row = lax.broadcasted_iota(jnp.int32, (width, lanes), 1) // group
    causal = key_row <= query_row + span
    for a in range(parts):
        same = seg_key[a * SUB : a * SUB + width] == seg_query[:, a * lanes : (a + 1) * lanes]
        bias[a] = jnp.where(same & causal, 0.0, MASKED)

    low_half = lax.broadcasted_iota(jnp.int32, (rows * group, dim), 1) < dim // 2

    def prepare(jj, _):
        load(0, q_hbm, q_buf, jj).wait()
        load(1, g_hbm, g_buf, jj).wait()
        load(2, o_hbm, o_buf, jj).wait()
        q_pair = q_buf[jj].astype(jnp.float32)
        g_pair = g_buf[jj].astype(jnp.float32)
        o_pair = o_buf[jj].astype(jnp.float32)
        for c in range(2):
            heads = slice(c * group, (c + 1) * group)
            q_wide = q_pair[:, heads, :].reshape(rows * group, dim)
            g_wide = g_pair[:, heads, :].reshape(rows * group, dim)
            product = g_wide * o_pair[:, heads, :].reshape(rows * group, dim)
            product = product + pltpu.roll(product, dim // 2, 1)
            high = product.astype(jnp.bfloat16).astype(jnp.float32)
            terms = jnp.where(low_half, high, product - high)
            q_rows[2 * jj + c] = q_wide.astype(jnp.bfloat16)
            g_rows[2 * jj + c, :, :dim] = g_wide.astype(jnp.bfloat16)
            g_rows[2 * jj + c, :, dim:] = terms.astype(jnp.bfloat16)
        return 0

    lax.fori_loop(0, pairs, prepare, 0)

    def pair(jj, _):
        dq_pair = []
        for c in range(2):
            j = 2 * jj + c
            for h in range(1, halo + 1):
                @pl.when(me >= h)
                def _():
                    forward(h, j).wait_recv()

            q = q_rows[j]
            g_terms = g_rows[j]
            g = g_terms[:, :dim]
            k = jnp.concatenate([kv_prev[h - 1, j, 0] for h in range(halo, 0, -1)] + [kv_own[j, 0]], axis=0)
            v = jnp.concatenate([kv_prev[h - 1, j, 1] for h in range(halo, 0, -1)] + [kv_own[j, 1]], axis=0)
            v = jnp.concatenate([v, jnp.full(v.shape, -1.0, v.dtype)], axis=1)
            pieces = (span + rows) // SUB
            dk = [None] * pieces
            dv = [None] * pieces
            dq = []
            for a in range(parts):
                q_a = q[a * lanes : (a + 1) * lanes]
                g_a = g[a * lanes : (a + 1) * lanes]
                k_a = k[a * SUB : a * SUB + width]
                v_a = v[a * SUB : a * SUB + width]
                raw = nt(k_a, q_a) + bias[a]
                top = jnp.max(raw, axis=0, keepdims=True)
                e = jnp.exp2((raw - top) * (scale * math.log2(math.e)))
                prob = e * (1.0 / jnp.sum(e, axis=0, keepdims=True))
                d_prob = nt(v_a, g_terms[a * lanes : (a + 1) * lanes])
                d_score = (prob * d_prob).astype(jnp.bfloat16)
                dv_a = nn(prob.astype(jnp.bfloat16), g_a)
                dk_a = nn(d_score, q_a)
                dq.append(tn(d_score, k_a) * scale)
                for b in range(width // SUB):
                    at = slice(b * SUB, (b + 1) * SUB)
                    dk[a + b] = dk_a[at] if dk[a + b] is None else dk[a + b] + dk_a[at]
                    dv[a + b] = dv_a[at] if dv[a + b] is None else dv[a + b] + dv_a[at]
            dq_pair.append(jnp.concatenate(dq, axis=0).reshape(rows, group, dim))
            for h in range(halo, -1, -1):
                at = slice((halo - h) * parts, (halo - h + 1) * parts)
                dk_h = jnp.concatenate(dk[at], axis=0) * scale
                dv_h = jnp.concatenate(dv[at], axis=0)
                if h:
                    back_out[h - 1, j, 0] = dk_h.astype(jnp.bfloat16)
                    back_out[h - 1, j, 1] = dv_h.astype(jnp.bfloat16)
                else:
                    own_sum[j, 0] = dk_h
                    own_sum[j, 1] = dv_h
            for h in range(1, halo + 1):
                @pl.when(me >= h)
                def _():
                    backward(h, j).start()
        dq_buf[jj] = jnp.concatenate(dq_pair, axis=1).astype(jnp.bfloat16)
        store(jj).start()
        return 0

    lax.fori_loop(0, pairs, pair, 0)

    for j in range(kv_heads):
        for h in range(1, halo + 1):
            @pl.when(me + h < devices)
            def _():
                backward(h, j).wait_recv()
                own_sum[j] = own_sum[j] + back_in[h - 1, j].astype(jnp.float32)
        for which in range(2):
            flat[which, pl.ds(j, rows, stride=kv_heads), :] = own_sum[j, which]
    last = [
        pltpu.make_async_copy(kv_raw.at[0], dk_hbm, kv_sem.at[0]),
        pltpu.make_async_copy(kv_raw.at[1], dv_hbm, kv_sem.at[1]),
    ]
    for which in range(2):
        kv_raw[which] = flat[which].reshape(rows, kv_heads, dim).astype(jnp.bfloat16)
        last[which].start()

    for jj in range(pairs):
        store(jj).wait()
    for j in range(kv_heads):
        for h in range(1, halo + 1):
            @pl.when(me + h < devices)
            def _():
                forward(h, j).wait_send()

            @pl.when(me >= h)
            def _():
                backward(h, j).wait_send()
    for copy in last:
        copy.wait()


def write(dq_in, dk_in, dv_in, dq_out, dk_out, dv_out, dq_buf, kv_buf, in_sem, out_sem):
    rows = dq_in.shape[0]
    step = rows // PARTS
    routes = [
        (dq_in.at[pl.ds(c * step, step)], dq_buf.at[pl.ds(c * step, step)], dq_out.at[pl.ds(c * step, step)])
        for c in range(PARTS)
    ]
    routes.append((dk_in, kv_buf.at[0], dk_out))
    routes.append((dv_in, kv_buf.at[1], dv_out))
    loads = [pltpu.make_async_copy(a, b, in_sem.at[n]) for n, (a, b, _) in enumerate(routes)]
    stores = [pltpu.make_async_copy(b, c, out_sem.at[n]) for n, (_, b, c) in enumerate(routes)]
    for copy in loads:
        copy.start()
    for load, store in zip(loads, stores):
        load.wait()
        store.start()
    for copy in stores:
        copy.wait()


def shards(queries, keys, values, outputs, out_grad, segments):
    ctx_count, head_count = lax.axis_size("ctx"), lax.axis_size("head")
    rows, q_heads, dim = queries.shape
    kv_heads = keys.shape[1]
    group = q_heads // kv_heads
    halo = max(1, head_count // 4)
    pairs = kv_heads // 2
    width = halo * rows + SUB
    sizes = (ctx_count, head_count, halo, rows, kv_heads, group, dim)
    lines = segments.reshape(ctx_count * head_count, rows)
    bf16, f32 = jnp.bfloat16, jnp.float32
    big = pltpu.VMEM((pairs, rows, 2 * group, dim), bf16)
    hbm = pl.BlockSpec(memory_space=pl.ANY)
    limit = 56 * 1024 * 1024
    work = rows * q_heads * (halo + 1) * rows
    shapes = (
        jax.ShapeDtypeStruct(queries.shape, bf16),
        jax.ShapeDtypeStruct(keys.shape, bf16),
        jax.ShapeDtypeStruct(values.shape, bf16),
    )
    grads = pl.pallas_call(
        functools.partial(kernel, sizes),
        out_shape=shapes,
        in_specs=[hbm] * 6,
        out_specs=(hbm,) * 3,
        scratch_shapes=[
            big, big, big, big,
            pltpu.VMEM((kv_heads, rows * group, dim), bf16),
            pltpu.VMEM((kv_heads, rows * group, 2 * dim), bf16),
            pltpu.VMEM((2, rows, kv_heads, dim), bf16),
            pltpu.VMEM(lines.shape, jnp.int32),
            pltpu.VMEM((2, rows * kv_heads, dim), f32),
            pltpu.VMEM((kv_heads, 2, rows, dim), bf16),
            pltpu.VMEM((halo, kv_heads, 2, rows, dim), bf16),
            pltpu.VMEM((halo, kv_heads, 2, rows, dim), bf16),
            pltpu.VMEM((halo, kv_heads, 2, rows, dim), bf16),
            pltpu.VMEM((kv_heads, 2, rows, dim), f32),
            pltpu.VMEM((rows // SUB, width, SUB * group), f32),
            pltpu.SemaphoreType.DMA((3, pairs)),
            pltpu.SemaphoreType.DMA((pairs,)),
            pltpu.SemaphoreType.DMA((3,)),
            pltpu.SemaphoreType.DMA((halo, kv_heads)),
            pltpu.SemaphoreType.DMA((halo, kv_heads)),
            pltpu.SemaphoreType.DMA((halo, kv_heads)),
            pltpu.SemaphoreType.DMA((halo, kv_heads)),
        ],
        compiler_params=pltpu.CompilerParams(
            collective_id=0, has_side_effects=True, vmem_limit_bytes=limit
        ),
        cost_estimate=pl.CostEstimate(
            flops=10 * work * dim, bytes_accessed=8 * rows * q_heads * dim, transcendentals=work
        ),
    )(queries, keys, values, outputs, out_grad, lines)
    return pl.pallas_call(
        write,
        out_shape=shapes,
        in_specs=[hbm] * 3,
        out_specs=(hbm,) * 3,
        scratch_shapes=[
            pltpu.VMEM(queries.shape, bf16),
            pltpu.VMEM((2, *keys.shape), bf16),
            pltpu.SemaphoreType.DMA((PARTS + 2,)),
            pltpu.SemaphoreType.DMA((PARTS + 2,)),
        ],
        compiler_params=pltpu.CompilerParams(vmem_limit_bytes=limit),
    )(*grads)


def solution(mesh):
    tokens = P(("ctx", "head"), None, None)
    return jax.shard_map(
        shards,
        mesh=mesh,
        in_specs=(tokens, tokens, tokens, tokens, tokens, P()),
        out_specs=(tokens, tokens, tokens),
        check_vma=False,
    )
```

```python
import functools
import math

import jax
import jax.numpy as jnp
from jax import lax
from jax.experimental import pallas as pl
from jax.experimental.pallas import tpu as pltpu
from jax.sharding import PartitionSpec as P

SUB = 128
PARTS = 8
MASKED = -1e30
MESH = pl.DeviceIdType.MESH


def nt(a, b):
    return lax.dot_general(a, b, (((1,), (1,)), ((), ())), preferred_element_type=jnp.float32)


def nn(a, b):
    return jnp.dot(a, b, preferred_element_type=jnp.float32)


def tn(a, b):
    return lax.dot_general(a, b, (((0,), (0,)), ((), ())), preferred_element_type=jnp.float32)


def kernel(
    sizes,
    q_hbm, k_hbm, v_hbm, o_hbm, g_hbm, seg_hbm,
    dq_hbm, dk_hbm, dv_hbm,
    q_buf, g_buf, o_buf, dq_buf, q_rows, g_rows, kv_raw, seg_ref, flat, kv_own, kv_prev, back_out, back_in, own_sum, bias,
    in_sem, dq_sem, kv_sem, fwd_send, fwd_recv, bwd_send, bwd_recv,
):
    ctx_count, head_count, halo, rows, kv_heads, group, dim = sizes
    devices = ctx_count * head_count
    span = halo * rows
    pairs = kv_heads // 2
    wide = 2 * group
    lanes = SUB * group
    width = span + SUB
    parts = rows // SUB
    scale = dim ** (-0.5)
    me = lax.axis_index("ctx") * head_count + lax.axis_index("head")

    def device(i):
        return (i // head_count, i % head_count)

    def load(number, hbm, buf, jj):
        return pltpu.make_async_copy(
            hbm.at[:, pl.ds(jj * wide, wide), :], buf.at[jj], in_sem.at[number, jj]
        )

    def store(jj):
        return pltpu.make_async_copy(
            dq_buf.at[jj], dq_hbm.at[:, pl.ds(jj * wide, wide), :], dq_sem.at[jj]
        )

    def forward(h, j):
        return pltpu.make_async_remote_copy(
            src_ref=kv_own.at[j], dst_ref=kv_prev.at[h - 1, j],
            send_sem=fwd_send.at[h - 1, j], recv_sem=fwd_recv.at[h - 1, j],
            device_id=device(me + h), device_id_type=MESH,
        )

    def backward(h, j):
        return pltpu.make_async_remote_copy(
            src_ref=back_out.at[h - 1, j], dst_ref=back_in.at[h - 1, j],
            send_sem=bwd_send.at[h - 1, j], recv_sem=bwd_recv.at[h - 1, j],
            device_id=device(me - h), device_id_type=MESH,
        )

    first = [
        pltpu.make_async_copy(k_hbm, kv_raw.at[0], kv_sem.at[0]),
        pltpu.make_async_copy(v_hbm, kv_raw.at[1], kv_sem.at[1]),
        pltpu.make_async_copy(seg_hbm, seg_ref, kv_sem.at[2]),
    ]
    for copy in first:
        copy.start()
    barrier = pltpu.get_barrier_semaphore()
    for h in range(1, halo + 1):
        @pl.when(me >= h)
        def _():
            pl.semaphore_signal(barrier, inc=1, device_id=device(me - h), device_id_type=MESH)

        @pl.when(me + h < devices)
        def _():
            pl.semaphore_signal(barrier, inc=1, device_id=device(me + h), device_id_type=MESH)

    for jj in range(pairs):
        load(0, q_hbm, q_buf, jj).start()
        load(1, g_hbm, g_buf, jj).start()
        load(2, o_hbm, o_buf, jj).start()

    for which in range(2):
        first[which].wait()
        flat[which] = kv_raw[which].astype(jnp.float32).reshape(rows * kv_heads, dim)

    def split(j):
        for which in range(2):
            kv_own[j, which] = flat[which, pl.ds(j, rows, stride=kv_heads), :].astype(jnp.bfloat16)

    split(0)
    pl.semaphore_wait(barrier, jnp.minimum(me, halo) + jnp.minimum(devices - 1 - me, halo))

    for j in range(kv_heads):
        if j:
            split(j)
        for h in range(1, halo + 1):
            @pl.when(me + h < devices)
            def _():
                forward(h, j).start()

    for h in range(1, halo + 1):
        @pl.when(me < h)
        def _():
            kv_prev[h - 1] = jnp.zeros(kv_prev.shape[1:], kv_prev.dtype)

    first[2].wait()
    token = lax.broadcasted_iota(jnp.int32, (rows, rows * group), 0)
    lane = lax.broadcasted_iota(jnp.int32, (rows, rows * group), 1)
    spread = jnp.where(lane // group == token, 1.0, 0.0).astype(jnp.bfloat16)
    own_seg = seg_ref[pl.ds(me, 1), :].astype(jnp.float32)
    seg_query = nn(jnp.broadcast_to(own_seg, (8, rows)).astype(jnp.bfloat16), spread)[0:1]
    diagonal = lax.broadcasted_iota(jnp.int32, (rows, rows), 0) == lax.broadcasted_iota(
        jnp.int32, (rows, rows), 1
    )
    ones = jnp.ones((rows, lanes), jnp.bfloat16)
    columns = []
    for h in range(halo, -1, -1):
        line = seg_ref[pl.ds(jnp.maximum(me - h, 0), 1), :].astype(jnp.float32)
        line = jnp.where(me >= h, line, -1.0)
        column = jnp.where(diagonal, jnp.broadcast_to(line, (rows, rows)), 0.0)
        columns.append(nn(column.astype(jnp.bfloat16), ones))
    seg_key = jnp.concatenate(columns, axis=0)
    key_row = lax.broadcasted_iota(jnp.int32, (width, lanes), 0)
    query_row = lax.broadcasted_iota(jnp.int32, (width, lanes), 1) // group
    causal = key_row <= query_row + span
    for a in range(parts):
        same = seg_key[a * SUB : a * SUB + width] == seg_query[:, a * lanes : (a + 1) * lanes]
        bias[a] = jnp.where(same & causal, 0.0, MASKED)

    low_half = lax.broadcasted_iota(jnp.int32, (rows * group, dim), 1) < dim // 2

    def prepare(jj, _):
        load(0, q_hbm, q_buf, jj).wait()
        load(1, g_hbm, g_buf, jj).wait()
        load(2, o_hbm, o_buf, jj).wait()
        q_pair = q_buf[jj].astype(jnp.float32)
        g_pair = g_buf[jj].astype(jnp.float32)
        o_pair = o_buf[jj].astype(jnp.float32)
        for c in range(2):
            heads = slice(c * group, (c + 1) * group)
            q_wide = q_pair[:, heads, :].reshape(rows * group, dim)
            g_wide = g_pair[:, heads, :].reshape(rows * group, dim)
            product = g_wide * o_pair[:, heads, :].reshape(rows * group, dim)
            product = product + pltpu.roll(product, dim // 2, 1)
            high = product.astype(jnp.bfloat16).astype(jnp.float32)
            terms = jnp.where(low_half, high, product - high)
            q_rows[2 * jj + c] = q_wide.astype(jnp.bfloat16)
            g_rows[2 * jj + c, :, :dim] = g_wide.astype(jnp.bfloat16)
            g_rows[2 * jj + c, :, dim:] = terms.astype(jnp.bfloat16)
        return 0

    lax.fori_loop(0, pairs, prepare, 0)

    def pair(jj, _):
        dq_pair = []
        for c in range(2):
            j = 2 * jj + c
            for h in range(1, halo + 1):
                @pl.when(me >= h)
                def _():
                    forward(h, j).wait_recv()

            q = q_rows[j]
            g_terms = g_rows[j]
            g = g_terms[:, :dim]
            k = jnp.concatenate([kv_prev[h - 1, j, 0] for h in range(halo, 0, -1)] + [kv_own[j, 0]], axis=0)
            v = jnp.concatenate([kv_prev[h - 1, j, 1] for h in range(halo, 0, -1)] + [kv_own[j, 1]], axis=0)
            v = jnp.concatenate([v, jnp.full(v.shape, -1.0, v.dtype)], axis=1)
            pieces = (span + rows) // SUB
            dk = [None] * pieces
            dv = [None] * pieces
            dq = []
            for a in range(parts):
                q_a = q[a * lanes : (a + 1) * lanes]
                g_a = g[a * lanes : (a + 1) * lanes]
                k_a = k[a * SUB : a * SUB + width]
                v_a = v[a * SUB : a * SUB + width]
                raw = nt(k_a, q_a) + bias[a]
                top = jnp.max(raw, axis=0, keepdims=True)
                e = jnp.exp2((raw - top) * (scale * math.log2(math.e)))
                prob = e * (1.0 / jnp.sum(e, axis=0, keepdims=True))
                d_prob = nt(v_a, g_terms[a * lanes : (a + 1) * lanes])
                d_score = (prob * d_prob).astype(jnp.bfloat16)
                dv_a = nn(prob.astype(jnp.bfloat16), g_a)
                dk_a = nn(d_score, q_a)
                dq.append(tn(d_score, k_a) * scale)
                for b in range(width // SUB):
                    at = slice(b * SUB, (b + 1) * SUB)
                    dk[a + b] = dk_a[at] if dk[a + b] is None else dk[a + b] + dk_a[at]
                    dv[a + b] = dv_a[at] if dv[a + b] is None else dv[a + b] + dv_a[at]
            dq_pair.append(jnp.concatenate(dq, axis=0).reshape(rows, group, dim))
            for h in range(halo, -1, -1):
                at = slice((halo - h) * parts, (halo - h + 1) * parts)
                dk_h = jnp.concatenate(dk[at], axis=0) * scale
                dv_h = jnp.concatenate(dv[at], axis=0)
                if h:
                    back_out[h - 1, j, 0] = dk_h.astype(jnp.bfloat16)
                    back_out[h - 1, j, 1] = dv_h.astype(jnp.bfloat16)
                else:
                    own_sum[j, 0] = dk_h
                    own_sum[j, 1] = dv_h
            for h in range(1, halo + 1):
                @pl.when(me >= h)
                def _():
                    backward(h, j).start()
        dq_buf[jj] = jnp.concatenate(dq_pair, axis=1).astype(jnp.bfloat16)
        store(jj).start()
        return 0

    lax.fori_loop(0, pairs, pair, 0)

    for j in range(kv_heads):
        for h in range(1, halo + 1):
            @pl.when(me + h < devices)
            def _():
                backward(h, j).wait_recv()
                own_sum[j] = own_sum[j] + back_in[h - 1, j].astype(jnp.float32)
        for which in range(2):
            flat[which, pl.ds(j, rows, stride=kv_heads), :] = own_sum[j, which]
    last = [
        pltpu.make_async_copy(kv_raw.at[0], dk_hbm, kv_sem.at[0]),
        pltpu.make_async_copy(kv_raw.at[1], dv_hbm, kv_sem.at[1]),
    ]
    for which in range(2):
        kv_raw[which] = flat[which].reshape(rows, kv_heads, dim).astype(jnp.bfloat16)
        last[which].start()

    for jj in range(pairs):
        store(jj).wait()
    for j in range(kv_heads):
        for h in range(1, halo + 1):
            @pl.when(me + h < devices)
            def _():
                forward(h, j).wait_send()

            @pl.when(me >= h)
            def _():
                backward(h, j).wait_send()
    for copy in last:
        copy.wait()


def write(dq_in, dk_in, dv_in, dq_out, dk_out, dv_out, dq_buf, kv_buf, in_sem, out_sem):
    rows = dq_in.shape[0]
    step = rows // PARTS
    routes = [
        (dq_in.at[pl.ds(c * step, step)], dq_buf.at[pl.ds(c * step, step)], dq_out.at[pl.ds(c * step, step)])
        for c in range(PARTS)
    ]
    routes.append((dk_in, kv_buf.at[0], dk_out))
    routes.append((dv_in, kv_buf.at[1], dv_out))
    loads = [pltpu.make_async_copy(a, b, in_sem.at[n]) for n, (a, b, _) in enumerate(routes)]
    stores = [pltpu.make_async_copy(b, c, out_sem.at[n]) for n, (_, b, c) in enumerate(routes)]
    for copy in loads:
        copy.start()
    for load, store in zip(loads, stores):
        load.wait()
        store.start()
    for copy in stores:
        copy.wait()


def shards(queries, keys, values, outputs, out_grad, segments):
    ctx_count, head_count = lax.axis_size("ctx"), lax.axis_size("head")
    rows, q_heads, dim = queries.shape
    kv_heads = keys.shape[1]
    group = q_heads // kv_heads
    halo = max(1, head_count // 4)
    pairs = kv_heads // 2
    width = halo * rows + SUB
    sizes = (ctx_count, head_count, halo, rows, kv_heads, group, dim)
    lines = segments.reshape(ctx_count * head_count, rows)
    bf16, f32 = jnp.bfloat16, jnp.float32
    big = pltpu.VMEM((pairs, rows, 2 * group, dim), bf16)
    hbm = pl.BlockSpec(memory_space=pl.ANY)
    limit = 56 * 1024 * 1024
    work = rows * q_heads * (halo + 1) * rows
    shapes = (
        jax.ShapeDtypeStruct(queries.shape, bf16),
        jax.ShapeDtypeStruct(keys.shape, bf16),
        jax.ShapeDtypeStruct(values.shape, bf16),
    )
    grads = pl.pallas_call(
        functools.partial(kernel, sizes),
        out_shape=shapes,
        in_specs=[hbm] * 6,
        out_specs=(hbm,) * 3,
        scratch_shapes=[
            big, big, big, big,
            pltpu.VMEM((kv_heads, rows * group, dim), bf16),
            pltpu.VMEM((kv_heads, rows * group, 2 * dim), bf16),
            pltpu.VMEM((2, rows, kv_heads, dim), bf16),
            pltpu.VMEM(lines.shape, jnp.int32),
            pltpu.VMEM((2, rows * kv_heads, dim), f32),
            pltpu.VMEM((kv_heads, 2, rows, dim), bf16),
            pltpu.VMEM((halo, kv_heads, 2, rows, dim), bf16),
            pltpu.VMEM((halo, kv_heads, 2, rows, dim), bf16),
            pltpu.VMEM((halo, kv_heads, 2, rows, dim), bf16),
            pltpu.VMEM((kv_heads, 2, rows, dim), f32),
            pltpu.VMEM((rows // SUB, width, SUB * group), f32),
            pltpu.SemaphoreType.DMA((3, pairs)),
            pltpu.SemaphoreType.DMA((pairs,)),
            pltpu.SemaphoreType.DMA((3,)),
            pltpu.SemaphoreType.DMA((halo, kv_heads)),
            pltpu.SemaphoreType.DMA((halo, kv_heads)),
            pltpu.SemaphoreType.DMA((halo, kv_heads)),
            pltpu.SemaphoreType.DMA((halo, kv_heads)),
        ],
        compiler_params=pltpu.CompilerParams(
            collective_id=0, has_side_effects=True, vmem_limit_bytes=limit
        ),
        cost_estimate=pl.CostEstimate(
            flops=10 * work * dim, bytes_accessed=8 * rows * q_heads * dim, transcendentals=work
        ),
    )(queries, keys, values, outputs, out_grad, lines)
    return pl.pallas_call(
        write,
        out_shape=shapes,
        in_specs=[hbm] * 3,
        out_specs=(hbm,) * 3,
        scratch_shapes=[
            pltpu.VMEM(queries.shape, bf16),
            pltpu.VMEM((2, *keys.shape), bf16),
            pltpu.SemaphoreType.DMA((PARTS + 2,)),
            pltpu.SemaphoreType.DMA((PARTS + 2,)),
        ],
        compiler_params=pltpu.CompilerParams(vmem_limit_bytes=limit),
    )(*grads)


def solution(mesh):
    tokens = P(("ctx", "head"), None, None)
    return jax.shard_map(
        shards,
        mesh=mesh,
        in_specs=(tokens, tokens, tokens, tokens, tokens, P()),
        out_specs=(tokens, tokens, tokens),
        check_vma=False,
    )
```
